512 devices in a mesh: row: 8 (over z_hi, core), col: 64 (over y, x, z_lo).
Axes of the slice: x: 4, y: 8, z: 8 (z_hi: 4, z_lo: 2; z = z_hi * 2 + z_lo), core: 2. Of those that a mesh axis runs over, the one named last changes fastest.
Arguments:
- matrix: float32 [8, 8, 256, 16384], P(None, 'row', None, 'col'), may hold values from -7.5 to 7.5, as said below
Outputs:
- reduced: float32 [8, 8, 256, 16384], P(None, 'row', None, 'col')
The draws below stay inside these ranges and needn't reach their ends.
Inputs may be any that keep to these rules, and one draw needn't show every extreme that they name: The stored order-16384 matrix equals its transpose.
All inputs are finite; a program needn't handle non-finite values.
Results may differ from the reference program's by a relative error of at most 0.00015.
Values sent between devices are 32-bit elements; how exact they have to be, the bound alone decides.
A program may use at most 64 MiB of HBM per device.

```python
import jax
import jax.numpy as jnp
from jax import lax

BLK = 256
STEPS = 1
ORDER = 16384
RBLK = 8
N_ROW = 8


def draw_matrix(key, part):
    key = jax.random.fold_in(key, 11)
    first_key = jax.random.fold_in(key, 0)
    third_key = jax.random.fold_in(key, 2)
    ratio = (1.5 * (ORDER - 2 * BLK) / BLK) ** 0.5
    blocks = jnp.arange(ORDER, dtype=jnp.int32) // BLK
    below = (blocks[:, None] == blocks[None, :] + 1) & (blocks[None, :] <= 1)
    paired = below | below.T
    strong = 2.2 * jnp.clip(jax.random.normal(third_key, (ORDER, ORDER), jnp.float32), -3.4, 3.4)
    level = 2.2
    entries = jnp.clip(jax.random.normal(first_key, (ORDER, ORDER), jnp.float32), -4.0, 4.0)
    background = (entries + entries.T) * (0.70710678 * level / ratio)
    lower_part = jnp.where(below, strong, 0.0)
    dominant = lower_part + lower_part.T
    symmetric = jnp.where(paired, dominant, background)
    return symmetric.reshape(RBLK, N_ROW, BLK, ORDER)


def setup_inputs(seed: int = 0) -> dict:
    key_of = jax.random.split(jax.random.key(seed), 2)
    matrix = draw_matrix(jax.random.fold_in(key_of[1], 71), 0)
    return dict(matrix=matrix)


def exact_dot(left, right):
    return jnp.dot(left.astype(jnp.float32), right.astype(jnp.float32), precision=lax.Precision.HIGHEST, preferred_element_type=jnp.float32)

def reference(matrix):
    whole = matrix.reshape(ORDER, ORDER)
    identity = jnp.eye(BLK, dtype=jnp.float32)
    for step_index in range(STEPS):
        start = step_index * BLK
        split = start + BLK
        panel = whole[split:, start:split]
        gram = exact_dot(panel.T, panel)
        lower = jnp.linalg.cholesky(gram)
        lower_inv = jax.scipy.linalg.solve_triangular(lower, identity, lower=True)
        basis = exact_dot(panel, lower_inv.T)
        reflect = (-basis).at[:BLK].add(identity)
        kernel = jnp.linalg.inv(identity - basis[:BLK].T)
        trailing = whole[split:, split:]
        image = exact_dot(trailing, reflect)
        curvature = exact_dot(reflect.T, image)
        inner = exact_dot(exact_dot(kernel.T, curvature), kernel)
        twist = exact_dot(image, kernel) - 0.5 * exact_dot(reflect, inner)
        trailing = trailing - exact_dot(reflect, twist.T) - exact_dot(twist, reflect.T)
        whole = whole.at[split:, split:].set(trailing)
        band = jnp.zeros_like(panel).at[:BLK].set(lower.T)
        whole = whole.at[split:, start:split].set(band)
        whole = whole.at[start:split, split:].set(band.T)
    return whole.reshape(matrix.shape)
```

```python
import functools

import jax
import jax.numpy as jnp
from jax import lax
from jax.experimental import pallas as pl
from jax.experimental.pallas import tpu as pltpu
from jax.sharding import PartitionSpec as P

NY, NX, NZ, NL, NC = 8, 4, 4, 2, 2
W = 256
SUB = 32
QR = W // 4
F32, BF16 = jnp.float32, jnp.bfloat16
MESH = pl.DeviceIdType.MESH
VMEM_LIMIT = 48 * 1024 * 1024
NN = (((1,), (0,)), ((), ()))
NT = (((1,), (1,)), ((), ()))
TN = (((0,), (0,)), ((), ()))


def split2(v):
    hi = v.astype(BF16)
    return hi, (v - hi.astype(F32)).astype(BF16)


def split3(v):
    a = v.astype(BF16)
    rest = v - a.astype(F32)
    b = rest.astype(BF16)
    return a, b, (rest - b.astype(F32)).astype(BF16)


def mm(a, b, dims):
    return lax.dot_general(a, b, dims, preferred_element_type=F32)


def dot3(a, b, dims=NN):
    ah, al = split2(a)
    bh, bl = split2(b)
    return mm(ah, bh, dims) + (mm(ah, bl, dims) + mm(al, bh, dims))


def dot6(a, b, dims=NN):
    a1, a2, a3 = split3(a)
    b1, b2, b3 = split3(b)
    low = mm(a2, b2, dims) + (mm(a1, b3, dims) + mm(a3, b1, dims))
    return mm(a1, b1, dims) + ((mm(a1, b2, dims) + mm(a2, b1, dims)) + low)


def packed_tdot(a, b):
    a1, a2, a3 = split3(a)
    b1, b2, b3 = split3(b)
    left = jnp.concatenate([a1, a1, a2, a2, a1, a3], axis=0)
    right = jnp.concatenate([b1, b2, b1, b2, b3, b1], axis=0)
    return mm(left, right, TN)


def iota(shape, dim):
    return lax.broadcasted_iota(jnp.int32, shape, dim)


class Place:
    def __init__(self):
        self.r = lax.axis_index("row")
        self.c = lax.axis_index("col")
        self.z, self.h = self.r // NC, self.r % NC
        self.y, self.x, self.l = self.c // (NX * NL), (self.c // NL) % NX, self.c % NL
        self.piece = self.h * NZ + self.z
        self.native = self.l == self.h
        self.diag = jnp.logical_and(self.native, self.x == self.z)

    def at_y(self, d):
        return (self.r, ((self.y + d) % NY * NX + self.x) * NL + self.l)

    def at_x(self, d):
        return (self.r, (self.y * NX + (self.x + d) % NX) * NL + self.l)

    def at_l(self):
        return (self.r, (self.y * NX + self.x) * NL + (1 - self.l))

    def at_z(self, d):
        return (((self.z + d) % NZ) * NC + self.h, self.c)

    def at_core(self):
        return (self.z * NC + (1 - self.h), self.c)

    def at_row(self, d):
        return ((self.r + d) % (NZ * NC), self.c)


def rcopy(src, dst, send, recv, device):
    return pltpu.make_async_remote_copy(
        src_ref=src, dst_ref=dst, send_sem=send, recv_sem=recv, device_id=device, device_id_type=MESH
    )


def greet(devices):
    barrier = pltpu.get_barrier_semaphore()
    for device in devices:
        pl.semaphore_signal(barrier, inc=1, device_id=device, device_id_type=MESH)
    pl.semaphore_wait(barrier, len(devices))


def loop(n, body):
    def step(t, carry):
        body(t)
        return carry

    lax.fori_loop(0, n, step, 0)


class Spread:
    def __init__(self, place, buf, recv, send_x, send_y, send_l):
        self.p, self.buf, self.recv = place, buf, recv
        self.send_x, self.send_y, self.send_l = send_x, send_y, send_l

    def chunk(self, i, q):
        return self.buf.at[i, pl.ds(pl.multiple_of(q * QR, QR), QR)]

    def copy(self, i, q, send, device):
        part = self.chunk(i, q)
        return rcopy(part, part, send, self.recv.at[i, q], device)

    def to_x(self, d, q):
        return self.copy(self.p.y, q, self.send_x.at[d - 1, q], self.p.at_x(d))

    def to_y(self, side, s, q):
        sign = 1 if side == 0 else -1
        i = (self.p.y - sign * s + NY) % NY
        return self.copy(i, q, self.send_y.at[side, s, q], self.p.at_y(sign + NY))

    def to_l(self, i, q):
        return self.copy(i, q, self.send_l.at[i, q], self.p.at_l())

    def arrive(self, i, q):
        self.copy(i, q, self.send_l.at[i, q], self.p.at_l()).wait_recv()

    def own(self, home):
        p = self.p

        def body(q):
            @pl.when(jnp.logical_and(p.native, jnp.logical_not(home)))
            def _():
                self.arrive(p.y, q)

            @pl.when(jnp.logical_and(jnp.logical_not(p.native), q < 2))
            def _():
                self.arrive(p.y, q)

            @pl.when(p.diag)
            def _():
                for d in (1, 3, 2):
                    self.to_x(d, q).start()

            @pl.when(p.native)
            def _():
                self.to_l(p.y, q).start()

            @pl.when(jnp.logical_or(p.native, q < 2))
            def _():
                self.to_y(0, 0, q).start()
                self.to_y(1, 0, q).start()

        loop(4, body)

    def sends_y(self, side, s, q):
        if s < 3:
            return jnp.logical_or(self.p.native, q < 2)
        if side == 0:
            return q < jnp.where(self.p.native, 2, 1)
        return jnp.where(self.p.native, q // 2 == 1, q == 1)

    def ring(self, s):
        p = self.p
        for side in (0, 1):
            sign = 1 if side == 0 else -1
            i = (p.y - sign * s + NY) % NY

            def body(q, side=side, i=i):
                @pl.when(jnp.logical_or(p.native, q < 2))
                def _():
                    self.arrive(i, q)

                @pl.when(self.sends_y(side, s, q))
                def _():
                    self.to_y(side, s, q).start()

                @pl.when(jnp.logical_and(p.native, q >= 2))
                def _():
                    self.to_l(i, q).start()

            loop(4, body)

    def last(self):
        p = self.p
        i = (p.y + 4) % NY

        def body(q):
            @pl.when(jnp.logical_or(p.native, q < 2))
            def _():
                self.arrive(i, q)

            @pl.when(jnp.logical_and(p.native, q >= 2))
            def _():
                self.to_l(i, q).start()

        loop(4, body)

        @pl.when(jnp.logical_not(p.native))
        def _():
            def late(t):
                self.arrive(t // 2, 2 + t % 2)

            loop(2 * NY, late)

    def drain(self):
        p = self.p

        def body(q):
            @pl.when(p.diag)
            def _():
                for d in (1, 2, 3):
                    self.to_x(d, q).wait_send()

            for s in range(4):
                for side in (0, 1):

                    @pl.when(self.sends_y(side, s, q))
                    def _(s=s, side=side):
                        self.to_y(side, s, q).wait_send()

            @pl.when(p.native)
            def _():
                self.to_l(p.y, q).wait_send()

            @pl.when(jnp.logical_and(p.native, q >= 2))
            def _():
                def others(t):
                    self.to_l((p.y + 1 + t) % NY, q).wait_send()

                loop(NY - 1, others)

        loop(4, body)


SPREAD_SEMS = [
    pltpu.SemaphoreType.DMA((NY, 4)),
    pltpu.SemaphoreType.DMA((3, 4)),
    pltpu.SemaphoreType.DMA((2, 4, 4)),
    pltpu.SemaphoreType.DMA((NY, 4)),
]


class RowGather:
    def __init__(self, place, buf, lo, hi, recv, send):
        self.p, self.buf, self.lo, self.hi = place, buf, lo, hi
        self.recv, self.send = recv, send

    def copy(self, j, slot, device):
        part = self.buf.at[pl.ds(self.lo, self.hi - self.lo), j]
        return rcopy(part, part, self.send.at[slot], self.recv.at[j], device)

    def to_z(self, d):
        return self.copy(self.p.piece, d - 1, self.p.at_z(d))

    def to_core(self, d):
        j = self.p.h * NZ + (self.p.z - d + NZ) % NZ
        return self.copy(j, 3 + d, self.p.at_core())

    def start(self):
        for d in (1, 3, 2):
            self.to_z(d).start()
        self.to_core(0).start()

    def relay(self):
        for d in (1, 3, 2):
            self.to_core(d).wait_recv()
            self.to_core(d).start()

    def finish(self):
        for d in range(4):
            j = (1 - self.p.h) * NZ + (self.p.z - d + NZ) % NZ
            self.copy(j, 3 + d, self.p.at_core()).wait_recv()
        for d in (1, 2, 3):
            self.to_z(d).wait_send()
        for d in range(4):
            self.to_core(d).wait_send()


GATHER_SEMS = [pltpu.SemaphoreType.DMA((NZ * NC,)), pltpu.SemaphoreType.DMA((7,))]


def row_piece(r):
    return (r % NC) * NZ + r // NC


class RowScatter:
    def __init__(self, place, root, src, dst, recv, send):
        self.p, self.root, self.src, self.dst = place, root, src, dst
        self.recv, self.send = recv, send

    def copy(self, d):
        j = row_piece((self.p.r + d) % (NZ * NC))
        part = self.src.at[pl.ds(pl.multiple_of(j * SUB, SUB), SUB)]
        return rcopy(part, self.dst.at[j], self.send.at[d - 1], self.recv, self.p.at_row(d))

    def start(self):
        @pl.when(self.p.r == self.root)
        def _():
            for d in range(1, 8):
                self.copy(d).start()
            self.dst[self.p.piece] = self.src[pl.ds(pl.multiple_of(self.p.piece * SUB, SUB), SUB)]

    def arrive(self):
        @pl.when(self.p.r != self.root)
        def _():
            self.copy(1).wait_recv()

    def finish(self):
        @pl.when(self.p.r == self.root)
        def _():
            for d in range(1, 8):
                self.copy(d).wait_send()


SCATTER_SEMS = [pltpu.SemaphoreType.DMA(()), pltpu.SemaphoreType.DMA((7,))]

GRAM, PROD, FIRST, PANEL, NEXT = range(5)


def gather_kernel(a_ref, prow, agb, src, part, rb_core, sums, rb_z, *sems):
    sp_sems, ge, gl, sc3, sc4, sc2, zs, ar = (
        sems[0:4], sems[4:6], sems[6:8], sems[8:10], sems[10:12], sems[12:14], sems[14], sems[15:19])
    p = Place()
    greet([p.at_row(d) for d in range(1, 8)] + [p.at_y(1), p.at_y(NY - 1), p.at_l()]
          + [p.at_x(d) for d in (1, 2, 3)])

    spread = Spread(p, prow, *sp_sems)
    home_row = p.x * NC + p.l
    home = jnp.logical_and(p.diag, p.r == 0)

    @pl.when(p.r == 0)
    def _():
        src[...] = jnp.where(p.c == 0, 0.0, a_ref[0])

    @pl.when(p.r == 1)
    def _():
        src[...] = a_ref[0]

    def to_home(q):
        rows = pl.ds(pl.multiple_of(q * QR, QR), QR)
        return rcopy(src.at[rows], prow.at[p.y, rows], zs.at[q], sp_sems[0].at[p.y, q], (home_row, p.c))

    @pl.when(home)
    def _():
        prow[p.y] = src[...]

    sends_home = jnp.logical_and(p.r == 0, home_row != 0)

    @pl.when(sends_home)
    def _():
        loop(4, lambda q: to_home(q).start())

    panel = RowScatter(p, 0, src, agb.at[PANEL], *sc3)
    following = RowScatter(p, 1, src, agb.at[NEXT], *sc4)
    panel.start()
    following.start()

    spread.own(home)
    panel.arrive()
    following.arrive()
    early = RowGather(p, agb, PANEL, NEXT + 1, *ge)
    early.start()
    spread.ring(1)
    spread.ring(2)
    early.relay()
    spread.ring(3)
    spread.last()

    first = RowScatter(p, 1, prow.at[0], agb.at[FIRST], *sc2)
    first.start()

    part[...] = jnp.zeros_like(part)

    def products(i):
        block = prow[i]
        bh, bl = split2(block)
        ah, al = split2(a_ref[i])
        gram = mm(bh, bh, NT) + (mm(bh, bl, NT) + mm(bl, bh, NT))
        prod = mm(bh, ah, NN) + (mm(bh, al, NN) + mm(bl, ah, NN))
        part[GRAM] += gram.reshape(8, SUB, W)
        part[PROD] += prod.reshape(8, SUB, W)

    loop(NY, products)

    send_c, recv_c, send_z, recv_z = ar
    out = rcopy(part.at[:, pl.ds(pl.multiple_of((1 - p.h) * NZ, NZ), NZ)], rb_core, send_c, recv_c, p.at_core())
    out.start()
    out.wait_recv()
    sums[...] = part[:, pl.ds(pl.multiple_of(p.h * NZ, NZ), NZ)] + rb_core[...]

    def to_z(d):
        return rcopy(sums.at[:, (p.z + d) % NZ], rb_z.at[d - 1], send_z.at[d - 1], recv_z.at[d - 1], p.at_z(d))

    for d in (1, 3, 2):
        to_z(d).start()
    total = sums[:, p.z]
    for d in (1, 3, 2):
        to_z(d).wait_recv()
        total = total + rb_z[d - 1]
    agb[GRAM, p.piece] = total[0]
    agb[PROD, p.piece] = total[1]
    first.arrive()
    late = RowGather(p, agb, GRAM, FIRST + 1, *gl)
    late.start()
    early.finish()
    late.relay()
    late.finish()

    out.wait_send()
    for d in (1, 2, 3):
        to_z(d).wait_send()
    for each in (panel, following, first):
        each.finish()

    @pl.when(sends_home)
    def _():
        loop(4, lambda q: to_home(q).wait_send())

    spread.drain()


def gather_call(slab):
    whole = pl.BlockSpec(memory_space=pltpu.VMEM)
    return pl.pallas_call(
        gather_kernel,
        out_shape=(jax.ShapeDtypeStruct((NY, W, W), F32), jax.ShapeDtypeStruct((5, 8, SUB, W), F32)),
        in_specs=[whole],
        out_specs=(whole, whole),
        scratch_shapes=[
            pltpu.VMEM((W, W), F32),
            pltpu.VMEM((2, 8, SUB, W), F32),
            pltpu.VMEM((2, NZ, SUB, W), F32),
            pltpu.VMEM((2, NZ, SUB, W), F32),
            pltpu.VMEM((3, 2, SUB, W), F32),
        ]
        + SPREAD_SEMS + GATHER_SEMS + GATHER_SEMS + SCATTER_SEMS * 3
        + [pltpu.SemaphoreType.DMA((4,))]
        + [pltpu.SemaphoreType.DMA(()), pltpu.SemaphoreType.DMA(()),
           pltpu.SemaphoreType.DMA((3,)), pltpu.SemaphoreType.DMA((3,))],
        compiler_params=pltpu.CompilerParams(
            collective_id=0, has_side_effects=True, vmem_limit_bytes=VMEM_LIMIT),
        name="gather_panel",
    )(slab)


def factor_steps(state, j):
    j0 = j * SUB
    rows = iota((SUB, 1), 0)
    panel = state["s"][j0:j0 + SUB, :]
    for t in range(SUB):
        col = panel[:, j0 + t:j0 + t + 1]
        inv = 1.0 / col[t:t + 1, :]
        factor = jnp.where(rows > t, col, 0.0)
        panel = panel - factor * (panel[t:t + 1, :] * inv)
        yield
    lanes = iota((SUB, W), 1)
    diag = jnp.sum(jnp.where(lanes == j0 + iota((SUB, W), 0), panel[:, :W], 0.0), axis=1, keepdims=True)
    panel = panel * (1.0 / jnp.sqrt(diag))
    upper = jnp.where(lanes >= j0 + iota((SUB, W), 0), panel[:, :W], 0.0)
    state["row"] = upper
    state["lt"][j0:j0 + SUB, :] = upper
    state["y"][j0:j0 + SUB, :] = panel[:, W:]
    if j < 7:
        whole = jnp.concatenate([upper, panel[:, W:]], axis=1)
        state["s"][j0 + SUB:, :] -= packed_tdot(upper[:, j0 + SUB:] if (j0 + SUB) % 128 == 0 else upper, whole)[
            (0 if (j0 + SUB) % 128 == 0 else j0 + SUB):, :]


def invert_steps(m_ref, row, j):
    j0 = j * SUB
    cols = slice(j0, j0 + SUB)
    m_ref[:, cols] += row.T
    lanes = iota((SUB, W), 1)
    rows = iota((SUB, W), 0)
    panel = m_ref[cols, :]
    for t in range(SUB):
        here = lanes == j0 + t
        col = panel[:, j0 + t:j0 + t + 1]
        inv = 1.0 / col[t:t + 1, :]
        pivot = jnp.where(here[t:t + 1, :], 1.0, panel[t:t + 1, :]) * inv
        panel = jnp.where(rows == t, pivot, jnp.where(here, 0.0, panel) - col * pivot)
        yield
    left = m_ref[:, cols].T
    keep = jnp.logical_and(iota((W, W), 1) >= j0, iota((W, W), 1) < j0 + SUB)
    m_ref[...] = jnp.where(keep, 0.0, m_ref[...]) - packed_tdot(left, panel)
    m_ref[cols, :] = panel


def solve_kernel(agb, lt, y_ref, k_ref, vt_ref, it_ref, image_ref, r_ref, curv_ref, s, m):
    p = Place()
    eye = (iota((W, W), 0) == iota((W, W), 1)).astype(F32)
    s[:, :W] = agb[GRAM].reshape(W, W)
    s[:, W:] = eye
    m[...] = -agb[FIRST].reshape(W, W)
    state = dict(s=s, lt=lt, y=y_ref)
    previous = None
    for j in range(9):
        ahead = factor_steps(state, j) if j < 8 else iter(())
        behind = invert_steps(m, previous, j - 1) if j > 0 else iter(())
        running = [behind, ahead]
        while running:
            for each in list(running):
                if next(each, running) is running:
                    running.remove(each)
        previous = state["row"]
    chol_t, inv, near = lt[...], y_ref[...], m[...]
    panel = agb[PANEL].reshape(W, W)
    shifted = jnp.where(p.c == 1, chol_t.T, 0.0) - panel
    vt = dot6(inv, shifted)
    it = agb[NEXT].reshape(W, W) - dot6(inv, agb[PROD].reshape(W, W))
    k_ref[...] = dot6(near, chol_t, NT)
    r_ref[...] = dot6(near, shifted)
    vt_ref[...] = vt
    it_ref[...] = it
    image_ref[...] = it.T
    mine = vt_ref[pl.ds(pl.multiple_of(p.piece * SUB, SUB), SUB), :]
    curv_ref[...] = dot6(mine, it, NT)


def solve_call(agb):
    whole = pl.BlockSpec(memory_space=pltpu.VMEM)
    square = jax.ShapeDtypeStruct((W, W), F32)
    return pl.pallas_call(
        solve_kernel,
        out_shape=(square,) * 7 + (jax.ShapeDtypeStruct((SUB, W), F32),),
        in_specs=[whole],
        out_specs=(whole,) * 8,
        scratch_shapes=[pltpu.VMEM((W, 2 * W), F32), pltpu.VMEM((W, W), F32)],
        compiler_params=pltpu.CompilerParams(vmem_limit_bytes=VMEM_LIMIT),
        name="solve_small",
    )(agb)


def image_kernel(image, curv, irow, cgather, s1, rb1, rb2, s2, rb3, s3, rb4, *sems):
    sp_sems, ge, c1, c2, c3, c4 = sems[0:4], sems[4:6], sems[6:8], sems[8:10], sems[10:12], sems[12:14]
    p = Place()
    greet([p.at_row(d) for d in range(1, 8)] + [p.at_y(d) for d in range(1, 8)] + [p.at_l()]
          + [p.at_x(d) for d in (1, 2, 3)])
    spread = Spread(p, irow, *sp_sems)

    @pl.when(p.diag)
    def _():
        irow[p.y] = image[...]

    def to_l():
        return rcopy(curv, rb1, c1[0], c1[1], p.at_l())

    def to_x(d):
        x = (p.x + d) % NX
        return rcopy(s1.at[pl.ds(pl.multiple_of(x * 8, 8), 8)], rb2.at[d - 1], c2[0].at[d - 1], c2[1].at[d - 1], p.at_x(d))

    def to_y(d):
        return rcopy(s2, rb3.at[d - 1], c3[0].at[d - 1], c3[1].at[d - 1], p.at_y(d))

    def back_x(d):
        rows = pl.ds(pl.multiple_of(p.x * 8, 8), 8)
        return rcopy(s3, rb4.at[rows], c4[0].at[d - 1], c4[1].at[d - 1], p.at_x(d))

    to_l().start()
    spread.own(p.diag)
    to_l().wait_recv()
    s1[...] = curv[...] + rb1[...]
    for d in (1, 2, 3):
        to_x(d).start()
    spread.ring(1)
    total = s1[pl.ds(pl.multiple_of(p.x * 8, 8), 8)]
    for d in (1, 2, 3):
        to_x(d).wait_recv()
        total = total + rb2[d - 1]
    s2[...] = total
    for d in range(1, 8):
        to_y(d).start()
    spread.ring(2)
    total = s2[...]
    for d in range(1, 8):
        to_y(d).wait_recv()
        total = total + rb3[d - 1]
    s3[...] = total
    for d in (1, 2, 3):
        back_x(d).start()
    rb4[pl.ds(pl.multiple_of(p.x * 8, 8), 8)] = total
    spread.ring(3)
    for d in (1, 2, 3):
        back_x(d).wait_recv()
    cgather[0, p.piece] = rb4[...]
    gather = RowGather(p, cgather, 0, 1, *ge)
    gather.start()
    spread.last()
    gather.relay()
    gather.finish()
    to_l().wait_send()
    for d in (1, 2, 3):
        to_x(d).wait_send()
        back_x(d).wait_send()
    for d in range(1, 8):
        to_y(d).wait_send()
    spread.drain()


def image_call(image, curv):
    whole = pl.BlockSpec(memory_space=pltpu.VMEM)
    dma = pltpu.SemaphoreType.DMA
    return pl.pallas_call(
        image_kernel,
        out_shape=(jax.ShapeDtypeStruct((NY, W, W), F32), jax.ShapeDtypeStruct((1, 8, SUB, W), F32)),
        in_specs=[whole, whole],
        out_specs=(whole, whole),
        scratch_shapes=[
            pltpu.VMEM((SUB, W), F32),
            pltpu.VMEM((SUB, W), F32),
            pltpu.VMEM((3, 8, W), F32),
            pltpu.VMEM((8, W), F32),
            pltpu.VMEM((7, 8, W), F32),
            pltpu.VMEM((8, W), F32),
            pltpu.VMEM((SUB, W), F32),
        ]
        + SPREAD_SEMS + GATHER_SEMS
        + [dma(()), dma(()), dma((3,)), dma((3,)), dma((7,)), dma((7,)), dma((3,)), dma((3,))],
        compiler_params=pltpu.CompilerParams(
            collective_id=1, has_side_effects=True, vmem_limit_bytes=VMEM_LIMIT),
        name="spread_image",
    )(image, curv)


def update_kernel(a_ref, prow, irow, lt, y_ref, k_ref, vt_ref, it_ref, r_ref, curv, out, s_ref, u_ref, rn_ref):
    p = Place()
    i = pl.program_id(0)

    @pl.when(i == 0)
    def _():
        kern = k_ref[...]
        inner = dot3(dot3(kern, curv[0].reshape(W, W), TN), kern)
        s = dot3(kern, it_ref[...], TN) - 0.5 * dot3(inner + inner.T, vt_ref[...])
        s_ref[...] = s
        uh, ul = split2(dot3(y_ref[...], s, TN))
        u_ref[0] = uh
        u_ref[1] = ul
        rh, rl = split2(r_ref[...])
        rn_ref[0] = rh
        rn_ref[1] = rl

    ph, plo = split2(prow[0])
    ih, il = split2(irow[0])
    first = mm(ph, u_ref[0], TN) + (mm(ph, u_ref[1], TN) + mm(plo, u_ref[0], TN))
    second = mm(ih, rn_ref[0], NN) + (mm(ih, rn_ref[1], NN) + mm(il, rn_ref[0], NN))
    b = i * (NZ * NC) + p.r
    res = a_ref[0] + (first - second)
    res = jnp.where(b == 1, res - s_ref[...], res)
    out[0] = res

    @pl.when(p.c == 0)
    def _():
        out[0] = jnp.where(b == 0, a_ref[0], jnp.where(b == 1, lt[...], 0.0))

    @pl.when(jnp.logical_and(p.c > 0, b == 0))
    def _():
        out[0] = jnp.where(p.c == 1, lt[...].T, 0.0)


def update_call(slab, prow, irow, lt, y, k, vt, it, r, curv):
    tile = pl.BlockSpec((1, W, W), lambda i: (i, 0, 0))
    square = pl.BlockSpec((W, W), lambda i: (0, 0))
    return pl.pallas_call(
        update_kernel,
        grid=(NY,),
        out_shape=jax.ShapeDtypeStruct((NY, W, W), F32),
        in_specs=[tile, tile, tile] + [square] * 6 + [pl.BlockSpec((1, 8, SUB, W), lambda i: (0, 0, 0, 0))],
        out_specs=tile,
        scratch_shapes=[pltpu.VMEM((W, W), F32), pltpu.VMEM((2, W, W), BF16), pltpu.VMEM((2, W, W), BF16)],
        compiler_params=pltpu.CompilerParams(vmem_limit_bytes=VMEM_LIMIT),
        name="update_rows",
    )(slab, prow, irow, lt, y, k, vt, it, r, curv)


def on_device(matrix):
    slab = matrix.reshape(NY, W, W)
    prow, agb = gather_call(slab)
    lt, y, k, vt, it, image, r, curv = solve_call(agb)
    irow, cgather = image_call(image, curv)
    out = update_call(slab, prow, irow, lt, y, k, vt, it, r, cgather)
    return out.reshape(matrix.shape)


def solution(mesh):
    return jax.shard_map(
        on_device,
        mesh=mesh,
        in_specs=(P(None, "row", None, "col"),),
        out_specs=P(None, "row", None, "col"),
        check_vma=False,
    )
```

```python
import functools

import jax
import jax.numpy as jnp
from jax import lax
from jax.experimental import pallas as pl
from jax.experimental.pallas import tpu as pltpu
from jax.sharding import PartitionSpec as P

NY, NX, NZ, NL, NC = 8, 4, 4, 2, 2
W = 256
SUB = 32
NQ = 8
QR = W // NQ
GROUP = 8
F32, BF16 = jnp.float32, jnp.bfloat16
MESH = pl.DeviceIdType.MESH
VMEM_LIMIT = 48 * 1024 * 1024
NN = (((1,), (0,)), ((), ()))
NT = (((1,), (1,)), ((), ()))
TN = (((0,), (0,)), ((), ()))


def split2(v):
    hi = v.astype(BF16)
    return hi, (v - hi.astype(F32)).astype(BF16)


def split3(v):
    a = v.astype(BF16)
    rest = v - a.astype(F32)
    b = rest.astype(BF16)
    return a, b, (rest - b.astype(F32)).astype(BF16)


def mm(a, b, dims):
    return lax.dot_general(a, b, dims, preferred_element_type=F32)


def dot3(a, b, dims=NN):
    ah, al = split2(a)
    bh, bl = split2(b)
    return mm(ah, bh, dims) + (mm(ah, bl, dims) + mm(al, bh, dims))


def dot6(a, b, dims=NN):
    a1, a2, a3 = split3(a)
    b1, b2, b3 = split3(b)
    low = mm(a2, b2, dims) + (mm(a1, b3, dims) + mm(a3, b1, dims))
    return mm(a1, b1, dims) + ((mm(a1, b2, dims) + mm(a2, b1, dims)) + low)


def packed_tdot(a, b):
    a1, a2, a3 = split3(a)
    b1, b2, b3 = split3(b)
    left = jnp.concatenate([a1, a1, a2, a2, a1, a3], axis=0)
    right = jnp.concatenate([b1, b2, b1, b2, b3, b1], axis=0)
    return mm(left, right, TN)


def iota(shape, dim):
    return lax.broadcasted_iota(jnp.int32, shape, dim)


class Place:
    def __init__(self):
        self.r = lax.axis_index("row")
        self.c = lax.axis_index("col")
        self.z, self.h = self.r // NC, self.r % NC
        self.y, self.x, self.l = self.c // (NX * NL), (self.c // NL) % NX, self.c % NL
        self.piece = self.h * NZ + self.z
        self.native = self.l == self.h
        self.diag = jnp.logical_and(self.native, self.x == self.z)

    def at_y(self, d):
        return (self.r, ((self.y + d) % NY * NX + self.x) * NL + self.l)

    def at_x(self, d):
        return (self.r, (self.y * NX + (self.x + d) % NX) * NL + self.l)

    def at_l(self):
        return (self.r, (self.y * NX + self.x) * NL + (1 - self.l))

    def at_z(self, d):
        return (((self.z + d) % NZ) * NC + self.h, self.c)

    def at_core(self):
        return (self.z * NC + (1 - self.h), self.c)

    def at_row(self, d):
        return ((self.r + d) % (NZ * NC), self.c)


def rcopy(src, dst, send, recv, device):
    return pltpu.make_async_remote_copy(
        src_ref=src, dst_ref=dst, send_sem=send, recv_sem=recv, device_id=device, device_id_type=MESH
    )


def greet(devices):
    barrier = pltpu.get_barrier_semaphore()
    for device in devices:
        pl.semaphore_signal(barrier, inc=1, device_id=device, device_id_type=MESH)
    pl.semaphore_wait(barrier, len(devices))


def loop(n, body):
    def step(t, carry):
        body(t)
        return carry

    lax.fori_loop(0, n, step, 0)


class Spread:
    def __init__(self, place, buf, recv, send_x, send_y, send_l):
        self.p, self.buf, self.recv = place, buf, recv
        self.send_x, self.send_y, self.send_l = send_x, send_y, send_l

    def chunk(self, i, q):
        return self.buf.at[i, pl.ds(pl.multiple_of(q * QR, QR), QR)]

    def copy(self, i, q, send, device):
        part = self.chunk(i, q)
        return rcopy(part, part, send, self.recv.at[i, q], device)

    def to_x(self, d, q):
        return self.copy(self.p.y, q, self.send_x.at[d - 1, q], self.p.at_x(d))

    def to_y(self, side, s, q):
        sign = 1 if side == 0 else -1
        i = (self.p.y - sign * s + NY) % NY
        return self.copy(i, q, self.send_y.at[side, s, q], self.p.at_y(sign + NY))

    def to_l(self, i, q):
        return self.copy(i, q, self.send_l.at[i, q], self.p.at_l())

    def arrive(self, i, q):
        self.copy(i, q, self.send_l.at[i, q], self.p.at_l()).wait_recv()

    def own(self, home):
        p = self.p

        def body(q):
            @pl.when(jnp.logical_and(p.native, jnp.logical_not(home)))
            def _():
                self.arrive(p.y, q)

            @pl.when(jnp.logical_and(jnp.logical_not(p.native), q < NQ // 2))
            def _():
                self.arrive(p.y, q)

            @pl.when(p.diag)
            def _():
                for d in (1, 3, 2):
                    self.to_x(d, q).start()

            @pl.when(p.native)
            def _():
                self.to_l(p.y, q).start()

            @pl.when(jnp.logical_or(p.native, q < NQ // 2))
            def _():
                self.to_y(0, 0, q).start()
                self.to_y(1, 0, q).start()

        loop(NQ, body)

    def sends_y(self, side, s, q):
        if s < 3:
            return jnp.logical_or(self.p.native, q < NQ // 2)
        if side == 0:
            return q < jnp.where(self.p.native, NQ // 2, NQ // 4)
        return jnp.where(self.p.native, q, (q % (NQ // 2)) * 2 * (q < NQ // 2)) >= NQ // 2

    def ring(self, s):
        p = self.p

        def body(q):
            for side in (0, 1):
                sign = 1 if side == 0 else -1
                i = (p.y - sign * s + NY) % NY

                @pl.when(jnp.logical_or(p.native, q < NQ // 2))
                def _(i=i):
                    self.arrive(i, q)

                @pl.when(self.sends_y(side, s, q))
                def _(side=side):
                    self.to_y(side, s, q).start()

                @pl.when(jnp.logical_and(p.native, q >= NQ // 2))
                def _(i=i):
                    self.to_l(i, q).start()

        loop(NQ, body)

    def last(self):
        p = self.p
        i = (p.y + 4) % NY

        def body(q):
            @pl.when(jnp.logical_or(p.native, q < NQ // 2))
            def _():
                self.arrive(i, q)

            @pl.when(jnp.logical_and(p.native, q >= NQ // 2))
            def _():
                self.to_l(i, q).start()

        loop(NQ, body)

        @pl.when(jnp.logical_not(p.native))
        def _():
            def late(t):
                self.arrive(t // (NQ // 2), NQ // 2 + t % (NQ // 2))

            loop(NQ // 2 * NY, late)

    def drain(self):
        p = self.p

        def body(q):
            @pl.when(p.diag)
            def _():
                for d in (1, 2, 3):
                    self.to_x(d, q).wait_send()

            for s in range(4):
                for side in (0, 1):

                    @pl.when(self.sends_y(side, s, q))
                    def _(s=s, side=side):
                        self.to_y(side, s, q).wait_send()

            @pl.when(p.native)
            def _():
                self.to_l(p.y, q).wait_send()

            @pl.when(jnp.logical_and(p.native, q >= NQ // 2))
            def _():
                def others(t):
                    self.to_l((p.y + 1 + t) % NY, q).wait_send()

                loop(NY - 1, others)

        loop(NQ, body)


SPREAD_SEMS = [
    pltpu.SemaphoreType.DMA((NY, NQ)),
    pltpu.SemaphoreType.DMA((3, NQ)),
    pltpu.SemaphoreType.DMA((2, 4, NQ)),
    pltpu.SemaphoreType.DMA((NY, NQ)),
]


class RowGather:
    def __init__(self, place, buf, lo, hi, recv, send):
        self.p, self.buf, self.lo, self.hi = place, buf, lo, hi
        self.recv, self.send = recv, send

    def copy(self, j, slot, device):
        part = self.buf.at[pl.ds(self.lo, self.hi - self.lo), j]
        return rcopy(part, part, self.send.at[slot], self.recv.at[j], device)

    def to_z(self, d):
        return self.copy(self.p.piece, d - 1, self.p.at_z(d))

    def to_core(self, d):
        j = self.p.h * NZ + (self.p.z - d + NZ) % NZ
        return self.copy(j, 3 + d, self.p.at_core())

    def start(self):
        for d in (1, 3, 2):
            self.to_z(d).start()
        self.to_core(0).start()

    def relay(self):
        for d in (1, 3, 2):
            self.to_core(d).wait_recv()
            self.to_core(d).start()

    def finish(self):
        for d in range(4):
            j = (1 - self.p.h) * NZ + (self.p.z - d + NZ) % NZ
            self.copy(j, 3 + d, self.p.at_core()).wait_recv()
        for d in (1, 2, 3):
            self.to_z(d).wait_send()
        for d in range(4):
            self.to_core(d).wait_send()


GATHER_SEMS = [pltpu.SemaphoreType.DMA((NZ * NC,)), pltpu.SemaphoreType.DMA((7,))]


def row_piece(r):
    return (r % NC) * NZ + r // NC


class RowScatter:
    def __init__(self, place, root, active, src, dst, recv, send):
        self.p, self.src, self.dst = place, src, dst
        self.recv, self.send = recv, send
        self.is_root = jnp.logical_and(place.r == root, active)
        self.is_leaf = jnp.logical_and(place.r != root, active)

    def copy(self, d):
        j = row_piece((self.p.r + d) % (NZ * NC))
        part = self.src.at[pl.ds(pl.multiple_of(j * SUB, SUB), SUB)]
        return rcopy(part, self.dst.at[j], self.send.at[d - 1], self.recv, self.p.at_row(d))

    def start(self):
        @pl.when(self.is_root)
        def _():
            for d in range(1, 8):
                self.copy(d).start()
            self.dst[self.p.piece] = self.src[pl.ds(pl.multiple_of(self.p.piece * SUB, SUB), SUB)]

    def arrive(self):
        @pl.when(self.is_leaf)
        def _():
            self.copy(1).wait_recv()

    def finish(self):
        @pl.when(self.is_root)
        def _():
            for d in range(1, 8):
                self.copy(d).wait_send()


SCATTER_SEMS = [pltpu.SemaphoreType.DMA(()), pltpu.SemaphoreType.DMA((7,))]

GRAM, FIRST, PROD, PANEL, NEXT = range(5)


class RowReduce:
    def __init__(self, place, part, rb_core, sums, rb_z, send_c, recv_c, send_z, recv_z):
        self.p, self.part, self.rb_core, self.sums, self.rb_z = place, part, rb_core, sums, rb_z
        self.send_z, self.recv_z = send_z, recv_z
        other = pl.ds(pl.multiple_of((1 - place.h) * NZ, NZ), NZ)
        self.out = rcopy(part.at[other], rb_core, send_c, recv_c, place.at_core())

    def to_z(self, d):
        p = self.p
        return rcopy(self.sums.at[(p.z + d) % NZ], self.rb_z.at[d - 1],
                     self.send_z.at[d - 1], self.recv_z.at[d - 1], p.at_z(d))

    def start(self):
        self.out.start()

    def across(self):
        self.out.wait_recv()
        mine = pl.ds(pl.multiple_of(self.p.h * NZ, NZ), NZ)
        self.sums[...] = self.part[mine] + self.rb_core[...]
        for d in (1, 3, 2):
            self.to_z(d).start()

    def total(self):
        total = self.sums[self.p.z]
        for d in (1, 3, 2):
            self.to_z(d).wait_recv()
            total = total + self.rb_z[d - 1]
        return total

    def finish(self):
        self.out.wait_send()
        for d in (1, 2, 3):
            self.to_z(d).wait_send()


REDUCE_BUFS = [
    pltpu.VMEM((8, SUB, W), F32),
    pltpu.VMEM((NZ, SUB, W), F32),
    pltpu.VMEM((NZ, SUB, W), F32),
    pltpu.VMEM((3, SUB, W), F32),
]
REDUCE_SEMS = [pltpu.SemaphoreType.DMA(()), pltpu.SemaphoreType.DMA(()),
               pltpu.SemaphoreType.DMA((3,)), pltpu.SemaphoreType.DMA((3,))]


class EarlyGram:
    def __init__(self, place, agb, gram, rb, send_r, recv_r, send_x, send_l, send_y, recv):
        self.p, self.agb, self.gram, self.rb = place, agb, gram, rb
        self.send_r, self.recv_r = send_r, recv_r
        self.send_x, self.send_l, self.send_y, self.recv = send_x, send_l, send_y, recv
        p = place
        self.root = p.c == 0
        self.on_x = jnp.logical_and(p.y == 0, p.l == 0)
        self.on_y = p.y == 0

    def scatter(self, d):
        j = row_piece((self.p.r + d) % (NZ * NC))
        return rcopy(self.gram.at[j], self.rb.at[d - 1], self.send_r.at[d - 1], self.recv_r.at[d - 1], self.p.at_row(d))

    def piece(self, send, device):
        part = self.agb.at[pl.ds(GRAM, 2), self.p.piece]
        return rcopy(part, part, send, self.recv, device)

    def to_x(self, d):
        return self.piece(self.send_x.at[d - 1], self.p.at_x(d))

    def to_l(self):
        return self.piece(self.send_l, self.p.at_l())

    def to_y(self, d):
        return self.piece(self.send_y.at[d - 1], self.p.at_y(d))

    def local(self, blocks):
        @pl.when(self.root)
        def _():
            self.gram[...] = jnp.zeros_like(self.gram)

            def add(i):
                block = blocks[i]
                block = jnp.where(jnp.logical_and(i == 0, self.p.r == 0), 0.0, block)
                self.gram[...] += dot3(block, block, TN).reshape(8, SUB, W)

            loop(NY, add)
            for d in range(1, 8):
                self.scatter(d).start()

    def along_x(self, first):
        @pl.when(self.root)
        def _():
            total = self.gram[self.p.piece]
            for d in range(1, 8):
                self.scatter(d).wait_recv()
                total = total + self.rb[d - 1]
            self.agb[GRAM, self.p.piece] = total
        first.arrive()

        @pl.when(self.root)
        def _():
            for d in (1, 3, 2):
                self.to_x(d).start()

    def along_l(self):
        @pl.when(jnp.logical_and(self.on_x, self.p.x != 0))
        def _():
            self.to_l().wait_recv()

        @pl.when(self.on_x)
        def _():
            self.to_l().start()

    def along_y(self):
        @pl.when(jnp.logical_and(self.on_y, self.p.l != 0))
        def _():
            self.to_l().wait_recv()

        @pl.when(self.on_y)
        def _():
            for d in (4, 3, 5, 2, 6, 1, 7):
                self.to_y(d).start()

    def arrive(self):
        @pl.when(jnp.logical_not(self.on_y))
        def _():
            self.to_l().wait_recv()

    def finish(self):
        @pl.when(self.root)
        def _():
            for d in range(1, 8):
                self.scatter(d).wait_send()
            for d in (1, 2, 3):
                self.to_x(d).wait_send()

        @pl.when(self.on_x)
        def _():
            self.to_l().wait_send()

        @pl.when(self.on_y)
        def _():
            for d in range(1, 8):
                self.to_y(d).wait_send()


EARLY_SEMS = [pltpu.SemaphoreType.DMA((7,)), pltpu.SemaphoreType.DMA((7,)), pltpu.SemaphoreType.DMA((3,)),
              pltpu.SemaphoreType.DMA(()), pltpu.SemaphoreType.DMA((7,)), pltpu.SemaphoreType.DMA(())]


def pivot(t, p0, p1, cols, lane, row, jordan):
    col = cols[0]
    inv = 1.0 / col[t:t + 1, :]
    r0 = jnp.where(lane[t:t + 1] == t, 1.0, p0[t:t + 1]) * inv
    r1 = p1[t:t + 1] * inv
    here = row == t
    apply = jnp.logical_not(here) if jordan else row > t
    factor = jnp.where(apply, col, 0.0)
    rest = []
    for other in cols[1:]:
        ro = other[t:t + 1] * inv
        new = other - factor * ro
        rest.append(jnp.where(here, ro, new) if jordan else new)
    p0 = jnp.where(jnp.logical_and(apply, lane == t), 0.0, p0) - factor * r0
    p1 = p1 - factor * r1
    if jordan:
        p0, p1 = jnp.where(here, r0, p0), jnp.where(here, r1, p1)
    return p0, p1, rest


def group_columns(p0, t):
    return [jnp.broadcast_to(p0[:, u:u + 1], (SUB, 128)) for u in range(t, t + GROUP)]


def turn(v):
    return jnp.concatenate([v[:, SUB:], v[:, :SUB]], axis=1)


def turn_store(ref, body, panel):
    out = turn(body)
    ref[:W - SUB, :] = out[SUB:]
    ref[W - SUB:, :] = turn(panel)


def sweep(j, t_ref, m_ref, row_ref, lt_ref):
    lane = iota((SUB, 128), 1)
    row = iota((SUB, 128), 0)
    lane2 = iota((SUB, W), 1)
    before = row_ref[...]
    m_left = m_ref[:, :128].T[:SUB] + before
    q0 = m_ref[:SUB, :128] + jnp.where(lane < SUB, jnp.concatenate(
        [before[:, :SUB].T, jnp.zeros((SUB, 128 - SUB), F32)], axis=1), 0.0)
    q1 = m_ref[:SUB, 128:]
    p0, p1 = t_ref[:SUB, :128], t_ref[:SUB, 128:]
    for t in range(SUB):
        if t % GROUP == 0:
            p_cols, q_cols = group_columns(p0, t), group_columns(q0, t)
        p0, p1, p_cols = pivot(t, p0, p1, p_cols, lane, row, False)
        q0, q1, q_cols = pivot(t, q0, q1, q_cols, lane, row, True)

    diag = jnp.sum(jnp.where(lane == row, p0, 0.0), axis=1, keepdims=True)
    scale = 1.0 / jnp.sqrt(diag)
    p0, p1 = p0 * scale, p1 * scale
    upper = jnp.where(lane >= row, p0, 0.0)
    inside = jnp.where(lane < row, p0, jnp.where(lane == row, scale, 0.0))
    table = jnp.concatenate([jnp.where(lane < SUB, inside, p0), p1], axis=1)
    live = jnp.logical_and(lane2 < SUB * (8 - j), lane2 >= 0)
    upper = jnp.where(live, jnp.concatenate([upper, p1], axis=1), 0.0)
    first = iota((W, W), 1) < SUB
    t_new = jnp.where(first, 0.0, t_ref[...]) - packed_tdot(jnp.where(lane2 < SUB, 0.0, upper), table)
    panel = jnp.concatenate([q0, q1], axis=1)
    m_new = jnp.where(first, 0.0, m_ref[...]) - packed_tdot(m_left, panel)

    @pl.when(j < 8)
    def _():
        turn_store(t_ref, t_new, table)
        row_ref[...] = upper
        lt_ref[pl.ds(pl.multiple_of(j * SUB, SUB), SUB), :] = pltpu.roll(upper, j * SUB, 1)

    @pl.when(j > 0)
    def _():
        turn_store(m_ref, m_new, panel)


class Sems:
    def __init__(self, refs):
        self.refs, self.at = refs, 0

    def take(self, group):
        self.at += len(group)
        return self.refs[self.at - len(group):self.at]


def panel_kernel(a_hbm, prow, lt, y_ref, k_ref, vt_ref, it_ref, image_ref, r_ref, curv_ref,
                 a_ref, agb, src, near_src, gram, gram_rb, m, row, part, rb_core, sums, rb_z, load, *refs):
    sems = Sems(refs)
    p = Place()

    def fetch(i):
        return pltpu.make_async_copy(a_hbm.at[i], a_ref.at[i], load.at[i])

    loop(NY, lambda i: fetch(i).start())
    greet([p.at_row(d) for d in range(1, 8)] + [p.at_y(d) for d in range(1, 8)] + [p.at_l()]
          + [p.at_x(d) for d in (1, 2, 3)])
    fetch(0).wait()

    spread_sems = sems.take(SPREAD_SEMS)
    spread = Spread(p, prow, *spread_sems)
    home_row = p.x * NC + p.l
    home = jnp.logical_and(p.diag, p.r == 0)

    @pl.when(p.r == 0)
    def _():
        src[...] = jnp.where(p.c == 0, 0.0, a_ref[0])

    @pl.when(p.r == 1)
    def _():
        src[...] = a_ref[0]

    home_sem = sems.take([0])[0]

    def to_home(q):
        rows = pl.ds(pl.multiple_of(q * QR, QR), QR)
        return rcopy(src.at[rows], prow.at[p.y, rows], home_sem.at[q], spread_sems[0].at[p.y, q], (home_row, p.c))

    @pl.when(home)
    def _():
        prow[p.y] = src[...]

    sends_home = jnp.logical_and(p.r == 0, home_row != 0)

    @pl.when(sends_home)
    def _():
        loop(NQ, lambda q: to_home(q).start())

    panel = RowScatter(p, 0, p.c >= 0, src, agb.at[PANEL], *sems.take(SCATTER_SEMS))
    following = RowScatter(p, 1, p.c >= 0, src, agb.at[NEXT], *sems.take(SCATTER_SEMS))
    first = RowScatter(p, 1, p.c == 0, near_src, agb.at[FIRST], *sems.take(SCATTER_SEMS))
    early = EarlyGram(p, agb, gram, gram_rb, *sems.take(EARLY_SEMS))
    columns = RowGather(p, agb, PANEL, NEXT + 1, *sems.take(GATHER_SEMS))
    grams = RowGather(p, agb, GRAM, FIRST + 1, *sems.take(GATHER_SEMS))
    prods = RowGather(p, agb, PROD, PROD + 1, *sems.take(GATHER_SEMS))
    reduce = RowReduce(p, part, rb_core, sums, rb_z, *sems.take(REDUCE_SEMS))

    panel.start()
    following.start()
    loop(NY - 1, lambda i: fetch(i + 1).wait())

    @pl.when(jnp.logical_and(p.r == 1, p.c == 0))
    def _():
        near_src[...] = a_ref[0].T

    first.start()
    early.local(a_ref)
    spread.own(home)
    early.along_x(first)
    panel.arrive()
    following.arrive()
    columns.start()
    spread.ring(1)
    early.along_l()
    spread.ring(2)
    early.along_y()
    columns.relay()
    spread.ring(3)
    early.arrive()
    grams.start()
    spread.last()
    columns.finish()
    grams.relay()

    part[...] = jnp.zeros_like(part)

    def products(i):
        part[...] += dot3(prow[i], a_ref[i]).reshape(8, SUB, W)

    loop(NY, products)
    reduce.start()
    grams.finish()

    y_ref[...] = agb[GRAM].reshape(W, W)
    m[...] = -agb[FIRST].reshape(W, W)
    row[...] = jnp.zeros_like(row)

    def step(j):
        sweep(j, y_ref, m, row, lt)

        @pl.when(j == 1)
        def _():
            reduce.across()

        @pl.when(j == 4)
        def _():
            agb[PROD, p.piece] = reduce.total()
            prods.start()

        @pl.when(j == 7)
        def _():
            prods.relay()

    loop(9, step)
    prods.finish()

    chol_t, inv, near = lt[...], y_ref[...], m[...]
    shifted = jnp.where(p.c == 1, chol_t.T, 0.0) - agb[PANEL].reshape(W, W)
    vt = dot6(inv, shifted)
    it = agb[NEXT].reshape(W, W) - dot6(inv, agb[PROD].reshape(W, W))
    k_ref[...] = dot6(near, chol_t, NT)
    r_ref[...] = dot6(near, shifted)
    vt_ref[...] = vt
    it_ref[...] = it
    image_ref[...] = it.T
    mine = vt_ref[pl.ds(pl.multiple_of(p.piece * SUB, SUB), SUB), :]
    curv_ref[...] = dot6(mine, it, NT)

    reduce.finish()
    early.finish()
    for each in (panel, following, first):
        each.finish()

    @pl.when(sends_home)
    def _():
        loop(NQ, lambda q: to_home(q).wait_send())

    spread.drain()


def panel_call(slab):
    whole = pl.BlockSpec(memory_space=pltpu.VMEM)
    square = jax.ShapeDtypeStruct((W, W), F32)
    dma = pltpu.SemaphoreType.DMA
    return pl.pallas_call(
        panel_kernel,
        out_shape=(jax.ShapeDtypeStruct((NY, W, W), F32),) + (square,) * 7 + (jax.ShapeDtypeStruct((SUB, W), F32),),
        in_specs=[pl.BlockSpec(memory_space=pl.ANY)],
        out_specs=(whole,) * 9,
        scratch_shapes=[
            pltpu.VMEM((NY, W, W), F32),
            pltpu.VMEM((5, 8, SUB, W), F32),
            pltpu.VMEM((W, W), F32),
            pltpu.VMEM((W, W), F32),
            pltpu.VMEM((8, SUB, W), F32),
            pltpu.VMEM((7, SUB, W), F32),
            pltpu.VMEM((W, W), F32),
            pltpu.VMEM((SUB, W), F32),
        ] + REDUCE_BUFS + [dma((NY,))]
        + SPREAD_SEMS + [dma((NQ,))] + SCATTER_SEMS * 3 + EARLY_SEMS + GATHER_SEMS * 3 + REDUCE_SEMS,
        compiler_params=pltpu.CompilerParams(
            collective_id=0, has_side_effects=True, vmem_limit_bytes=VMEM_LIMIT),
        name="panel_factors",
    )(slab)


def image_kernel(image, curv, irow, cgather, s1, rb1, rb2, s2, rb3, s3, rb4, *sems):
    sp_sems, ge, c1, c2, c3, c4 = sems[0:4], sems[4:6], sems[6:8], sems[8:10], sems[10:12], sems[12:14]
    p = Place()
    greet([p.at_row(d) for d in range(1, 8)] + [p.at_y(d) for d in range(1, 8)] + [p.at_l()]
          + [p.at_x(d) for d in (1, 2, 3)])
    spread = Spread(p, irow, *sp_sems)

    @pl.when(p.diag)
    def _():
        irow[p.y] = image[...]

    def to_l():
        return rcopy(curv, rb1, c1[0], c1[1], p.at_l())

    def to_x(d):
        x = (p.x + d) % NX
        return rcopy(s1.at[pl.ds(pl.multiple_of(x * 8, 8), 8)], rb2.at[d - 1], c2[0].at[d - 1], c2[1].at[d - 1], p.at_x(d))

    def to_y(d):
        return rcopy(s2, rb3.at[d - 1], c3[0].at[d - 1], c3[1].at[d - 1], p.at_y(d))

    def back_x(d):
        rows = pl.ds(pl.multiple_of(p.x * 8, 8), 8)
        return rcopy(s3, rb4.at[rows], c4[0].at[d - 1], c4[1].at[d - 1], p.at_x(d))

    to_l().start()
    spread.own(p.diag)
    to_l().wait_recv()
    s1[...] = curv[...] + rb1[...]
    for d in (1, 2, 3):
        to_x(d).start()
    spread.ring(1)
    total = s1[pl.ds(pl.multiple_of(p.x * 8, 8), 8)]
    for d in (1, 2, 3):
        to_x(d).wait_recv()
        total = total + rb2[d - 1]
    s2[...] = total
    for d in range(1, 8):
        to_y(d).start()
    spread.ring(2)
    total = s2[...]
    for d in range(1, 8):
        to_y(d).wait_recv()
        total = total + rb3[d - 1]
    s3[...] = total
    for d in (1, 2, 3):
        back_x(d).start()
    rb4[pl.ds(pl.multiple_of(p.x * 8, 8), 8)] = total
    spread.ring(3)
    for d in (1, 2, 3):
        back_x(d).wait_recv()
    cgather[0, p.piece] = rb4[...]
    gather = RowGather(p, cgather, 0, 1, *ge)
    gather.start()
    spread.last()
    gather.relay()
    gather.finish()
    to_l().wait_send()
    for d in (1, 2, 3):
        to_x(d).wait_send()
        back_x(d).wait_send()
    for d in range(1, 8):
        to_y(d).wait_send()
    spread.drain()


def image_call(image, curv):
    whole = pl.BlockSpec(memory_space=pltpu.VMEM)
    dma = pltpu.SemaphoreType.DMA
    return pl.pallas_call(
        image_kernel,
        out_shape=(jax.ShapeDtypeStruct((NY, W, W), F32), jax.ShapeDtypeStruct((1, 8, SUB, W), F32)),
        in_specs=[whole, whole],
        out_specs=(whole, whole),
        scratch_shapes=[
            pltpu.VMEM((SUB, W), F32),
            pltpu.VMEM((SUB, W), F32),
            pltpu.VMEM((3, 8, W), F32),
            pltpu.VMEM((8, W), F32),
            pltpu.VMEM((7, 8, W), F32),
            pltpu.VMEM((8, W), F32),
            pltpu.VMEM((SUB, W), F32),
        ]
        + SPREAD_SEMS + GATHER_SEMS
        + [dma(()), dma(()), dma((3,)), dma((3,)), dma((7,)), dma((7,)), dma((3,)), dma((3,))],
        compiler_params=pltpu.CompilerParams(
            collective_id=1, has_side_effects=True, vmem_limit_bytes=VMEM_LIMIT),
        name="spread_image",
    )(image, curv)


def update_kernel(a_ref, prow, irow, lt, y_ref, k_ref, vt_ref, it_ref, r_ref, curv, out, s_ref, u_ref, rn_ref):
    p = Place()
    i = pl.program_id(0)

    @pl.when(i == 0)
    def _():
        kern = k_ref[...]
        inner = dot3(dot3(kern, curv[0].reshape(W, W), TN), kern)
        s = dot3(kern, it_ref[...], TN) - 0.5 * dot3(inner + inner.T, vt_ref[...])
        s_ref[...] = s
        uh, ul = split2(dot3(y_ref[...], s, TN))
        u_ref[0] = uh
        u_ref[1] = ul
        rh, rl = split2(r_ref[...])
        rn_ref[0] = rh
        rn_ref[1] = rl

    ph, plo = split2(prow[0])
    ih, il = split2(irow[0])
    first = mm(ph, u_ref[0], TN) + (mm(ph, u_ref[1], TN) + mm(plo, u_ref[0], TN))
    second = mm(ih, rn_ref[0], NN) + (mm(ih, rn_ref[1], NN) + mm(il, rn_ref[0], NN))
    b = i * (NZ * NC) + p.r
    res = a_ref[0] + (first - second)
    res = jnp.where(b == 1, res - s_ref[...], res)
    out[0] = res

    @pl.when(p.c == 0)
    def _():
        out[0] = jnp.where(b == 0, a_ref[0], jnp.where(b == 1, lt[...], 0.0))

    @pl.when(jnp.logical_and(p.c > 0, b == 0))
    def _():
        out[0] = jnp.where(p.c == 1, lt[...].T, 0.0)


def update_call(slab, prow, irow, lt, y, k, vt, it, r, curv):
    tile = pl.BlockSpec((1, W, W), lambda i: (i, 0, 0))
    square = pl.BlockSpec((W, W), lambda i: (0, 0))
    return pl.pallas_call(
        update_kernel,
        grid=(NY,),
        out_shape=jax.ShapeDtypeStruct((NY, W, W), F32),
        in_specs=[tile, tile, tile] + [square] * 6 + [pl.BlockSpec((1, 8, SUB, W), lambda i: (0, 0, 0, 0))],
        out_specs=tile,
        scratch_shapes=[pltpu.VMEM((W, W), F32), pltpu.VMEM((2, W, W), BF16), pltpu.VMEM((2, W, W), BF16)],
        compiler_params=pltpu.CompilerParams(vmem_limit_bytes=VMEM_LIMIT),
        name="update_rows",
    )(slab, prow, irow, lt, y, k, vt, it, r, curv)


def on_device(matrix):
    slab = matrix.reshape(NY, W, W)
    prow, lt, y, k, vt, it, image, r, curv = panel_call(slab)
    irow, cgather = image_call(image, curv)
    out = update_call(slab, prow, irow, lt, y, k, vt, it, r, cgather)
    return out.reshape(matrix.shape)


def solution(mesh):
    return jax.shard_map(
        on_device,
        mesh=mesh,
        in_specs=(P(None, "row", None, "col"),),
        out_specs=P(None, "row", None, "col"),
        check_vma=False,
    )
```

```python
import functools

import jax
import jax.numpy as jnp
from jax import lax
from jax.experimental import pallas as pl
from jax.experimental.pallas import tpu as pltpu
from jax.sharding import PartitionSpec as P

NY, NX, NZ, NL, NC = 8, 4, 4, 2, 2
W = 256
SUB = 32
NQ = 8
QR = W // NQ
GROUP = 8
F32, BF16 = jnp.float32, jnp.bfloat16
MESH = pl.DeviceIdType.MESH
VMEM_LIMIT = 48 * 1024 * 1024
NN = (((1,), (0,)), ((), ()))
NT = (((1,), (1,)), ((), ()))
TN = (((0,), (0,)), ((), ()))


def split2(v):
    hi = v.astype(BF16)
    return hi, (v - hi.astype(F32)).astype(BF16)


def split3(v):
    a = v.astype(BF16)
    rest = v - a.astype(F32)
    b = rest.astype(BF16)
    return a, b, (rest - b.astype(F32)).astype(BF16)


def mm(a, b, dims):
    return lax.dot_general(a, b, dims, preferred_element_type=F32)


def dot3(a, b, dims=NN):
    ah, al = split2(a)
    bh, bl = split2(b)
    return mm(ah, bh, dims) + (mm(ah, bl, dims) + mm(al, bh, dims))


def dot6(a, b, dims=NN):
    a1, a2, a3 = split3(a)
    b1, b2, b3 = split3(b)
    low = mm(a2, b2, dims) + (mm(a1, b3, dims) + mm(a3, b1, dims))
    return mm(a1, b1, dims) + ((mm(a1, b2, dims) + mm(a2, b1, dims)) + low)


def packed_tdot(a, b):
    a1, a2, a3 = split3(a)
    b1, b2, b3 = split3(b)
    left = jnp.concatenate([a1, a1, a2, a2, a1, a3], axis=0)
    right = jnp.concatenate([b1, b2, b1, b2, b3, b1], axis=0)
    return mm(left, right, TN)


def iota(shape, dim):
    return lax.broadcasted_iota(jnp.int32, shape, dim)


class Place:
    def __init__(self):
        self.r = lax.axis_index("row")
        self.c = lax.axis_index("col")
        self.z, self.h = self.r // NC, self.r % NC
        self.y, self.x, self.l = self.c // (NX * NL), (self.c // NL) % NX, self.c % NL
        self.piece = self.h * NZ + self.z
        self.native = self.l == self.h
        self.diag = jnp.logical_and(self.native, self.x == self.z)

    def at_y(self, d):
        return (self.r, ((self.y + d) % NY * NX + self.x) * NL + self.l)

    def at_x(self, d):
        return (self.r, (self.y * NX + (self.x + d) % NX) * NL + self.l)

    def at_l(self):
        return (self.r, (self.y * NX + self.x) * NL + (1 - self.l))

    def at_z(self, d):
        return (((self.z + d) % NZ) * NC + self.h, self.c)

    def at_core(self):
        return (self.z * NC + (1 - self.h), self.c)

    def at_row(self, d):
        return ((self.r + d) % (NZ * NC), self.c)


def rcopy(src, dst, send, recv, device):
    return pltpu.make_async_remote_copy(
        src_ref=src, dst_ref=dst, send_sem=send, recv_sem=recv, device_id=device, device_id_type=MESH
    )


def greet(devices):
    barrier = pltpu.get_barrier_semaphore()
    for device in devices:
        pl.semaphore_signal(barrier, inc=1, device_id=device, device_id_type=MESH)
    pl.semaphore_wait(barrier, len(devices))


def loop(n, body):
    def step(t, carry):
        body(t)
        return carry

    lax.fori_loop(0, n, step, 0)


class Spread:
    def __init__(self, place, buf, recv, send_x, send_y, send_l):
        self.p, self.buf, self.recv = place, buf, recv
        self.send_x, self.send_y, self.send_l = send_x, send_y, send_l

    def chunk(self, i, q):
        return self.buf.at[i, pl.ds(pl.multiple_of(q * QR, QR), QR)]

    def copy(self, i, q, send, device):
        part = self.chunk(i, q)
        return rcopy(part, part, send, self.recv.at[i, q], device)

    def to_x(self, d, q):
        return self.copy(self.p.y, q, self.send_x.at[d - 1], self.p.at_x(d))

    def to_y(self, side, s, q):
        sign = 1 if side == 0 else -1
        i = (self.p.y - sign * s + NY) % NY
        return self.copy(i, q, self.send_y.at[side, s], self.p.at_y(sign + NY))

    def to_l(self, i, q):
        return self.copy(i, q, self.send_l.at[i], self.p.at_l())

    def arrive(self, i, q):
        self.copy(i, q, self.send_l.at[i], self.p.at_l()).wait_recv()

    def own(self, home, beside=lambda q: None):
        p = self.p

        def body(q):
            @pl.when(jnp.logical_and(p.native, jnp.logical_not(home)))
            def _():
                self.arrive(p.y, q)

            @pl.when(jnp.logical_and(jnp.logical_not(p.native), q < NQ // 2))
            def _():
                self.arrive(p.y, q)

            @pl.when(p.diag)
            def _():
                for d in (1, 3, 2):
                    self.to_x(d, q).start()

            @pl.when(p.native)
            def _():
                self.to_l(p.y, q).start()

            @pl.when(jnp.logical_or(p.native, q < NQ // 2))
            def _():
                self.to_y(0, 0, q).start()
                self.to_y(1, 0, q).start()

            beside(q)

        loop(NQ, body)

    def sends_y(self, side, s, q):
        if s < 3:
            return jnp.logical_or(self.p.native, q < NQ // 2)
        if side == 0:
            return q < jnp.where(self.p.native, NQ // 2, NQ // 4)
        return jnp.where(self.p.native, q, (q % (NQ // 2)) * 2 * (q < NQ // 2)) >= NQ // 2

    def ring(self, s):
        p = self.p

        def body(q):
            for side in (0, 1):
                sign = 1 if side == 0 else -1
                i = (p.y - sign * s + NY) % NY

                @pl.when(jnp.logical_or(p.native, q < NQ // 2))
                def _(i=i):
                    self.arrive(i, q)

                @pl.when(self.sends_y(side, s, q))
                def _(side=side):
                    self.to_y(side, s, q).start()

                @pl.when(jnp.logical_and(p.native, q >= NQ // 2))
                def _(i=i):
                    self.to_l(i, q).start()

        loop(NQ, body)

    def last(self):
        p = self.p
        i = (p.y + 4) % NY

        def body(q):
            @pl.when(jnp.logical_or(p.native, q < NQ // 2))
            def _():
                self.arrive(i, q)

            @pl.when(jnp.logical_and(p.native, q >= NQ // 2))
            def _():
                self.to_l(i, q).start()

        loop(NQ, body)

    def late(self, i):
        @pl.when(jnp.logical_not(self.p.native))
        def _():
            loop(NQ // 2, lambda q: self.arrive(i, NQ // 2 + q))

    def sent(self, rows, send):
        part = self.buf.at[self.p.y, pl.ds(0, rows)]
        rcopy(part, part, send, self.recv.at[0, 0], self.p.at_l()).wait_send()

    def drain(self):
        p = self.p

        @pl.when(p.diag)
        def _():
            for d in range(3):
                self.sent(W, self.send_x.at[d])

        def ring(full):
            for side in (0, 1):
                for s in range(3):
                    self.sent(full, self.send_y.at[side, s])
                self.sent(full // 2, self.send_y.at[side, 3])

        @pl.when(p.native)
        def _():
            ring(W)
            self.sent(W, self.send_l.at[p.y])
            loop(NY - 1, lambda t: self.sent(W // 2, self.send_l.at[(p.y + 1 + t) % NY]))

        @pl.when(jnp.logical_not(p.native))
        def _():
            ring(W // 2)


SPREAD_SEMS = [
    pltpu.SemaphoreType.DMA((NY, NQ)),
    pltpu.SemaphoreType.DMA((3,)),
    pltpu.SemaphoreType.DMA((2, 4)),
    pltpu.SemaphoreType.DMA((NY,)),
]


class RowGather:
    def __init__(self, place, buf, lo, hi, recv, send):
        self.p, self.buf, self.lo, self.hi = place, buf, lo, hi
        self.recv, self.send = recv, send

    def copy(self, j, slot, device):
        part = self.buf.at[pl.ds(self.lo, self.hi - self.lo), j]
        return rcopy(part, part, self.send.at[slot], self.recv.at[j], device)

    def to_z(self, d):
        return self.copy(self.p.piece, d - 1, self.p.at_z(d))

    def to_core(self, d):
        j = self.p.h * NZ + (self.p.z - d + NZ) % NZ
        return self.copy(j, 3 + d, self.p.at_core())

    def start(self):
        for d in (1, 3, 2):
            self.to_z(d).start()
        self.to_core(0).start()

    def relay(self):
        for d in (1, 3, 2):
            self.to_core(d).wait_recv()
            self.to_core(d).start()

    def finish(self):
        for d in range(4):
            j = (1 - self.p.h) * NZ + (self.p.z - d + NZ) % NZ
            self.copy(j, 3 + d, self.p.at_core()).wait_recv()
        for d in (1, 2, 3):
            self.to_z(d).wait_send()
        for d in range(4):
            self.to_core(d).wait_send()


GATHER_SEMS = [pltpu.SemaphoreType.DMA((NZ * NC,)), pltpu.SemaphoreType.DMA((7,))]


def row_piece(r):
    return (r % NC) * NZ + r // NC


class RowScatter:
    def __init__(self, place, root, active, src, dst, recv, send):
        self.p, self.src, self.dst = place, src, dst
        self.recv, self.send = recv, send
        self.is_root = jnp.logical_and(place.r == root, active)
        self.is_leaf = jnp.logical_and(place.r != root, active)

    def copy(self, d):
        j = row_piece((self.p.r + d) % (NZ * NC))
        part = self.src.at[pl.ds(pl.multiple_of(j * SUB, SUB), SUB)]
        return rcopy(part, self.dst.at[j], self.send.at[d - 1], self.recv, self.p.at_row(d))

    def start(self):
        @pl.when(self.is_root)
        def _():
            for d in range(1, 8):
                self.copy(d).start()
            self.dst[self.p.piece] = self.src[pl.ds(pl.multiple_of(self.p.piece * SUB, SUB), SUB)]

    def arrive(self):
        @pl.when(self.is_leaf)
        def _():
            self.copy(1).wait_recv()

    def finish(self):
        @pl.when(self.is_root)
        def _():
            for d in range(1, 8):
                self.copy(d).wait_send()


SCATTER_SEMS = [pltpu.SemaphoreType.DMA(()), pltpu.SemaphoreType.DMA((7,))]

GRAM, FIRST, PROD, PANEL, NEXT = range(5)


class RowReduce:
    def __init__(self, place, part, rb_core, sums, rb_z, send_c, recv_c, send_z, recv_z):
        self.p, self.part, self.rb_core, self.sums, self.rb_z = place, part, rb_core, sums, rb_z
        self.send_z, self.recv_z = send_z, recv_z
        other = pl.ds(pl.multiple_of((1 - place.h) * NZ, NZ), NZ)
        self.out = rcopy(part.at[other], rb_core, send_c, recv_c, place.at_core())

    def to_z(self, d):
        p = self.p
        return rcopy(self.sums.at[(p.z + d) % NZ], self.rb_z.at[d - 1],
                     self.send_z.at[d - 1], self.recv_z.at[d - 1], p.at_z(d))

    def start(self):
        self.out.start()

    def across(self):
        self.out.wait_recv()
        mine = pl.ds(pl.multiple_of(self.p.h * NZ, NZ), NZ)
        self.sums[...] = self.part[mine] + self.rb_core[...]
        for d in (1, 3, 2):
            self.to_z(d).start()

    def total(self):
        total = self.sums[self.p.z]
        for d in (1, 3, 2):
            self.to_z(d).wait_recv()
            total = total + self.rb_z[d - 1]
        return total

    def finish(self):
        self.out.wait_send()
        for d in (1, 2, 3):
            self.to_z(d).wait_send()


REDUCE_BUFS = [
    pltpu.VMEM((8, SUB, W), F32),
    pltpu.VMEM((NZ, SUB, W), F32),
    pltpu.VMEM((NZ, SUB, W), F32),
    pltpu.VMEM((3, SUB, W), F32),
]
REDUCE_SEMS = [pltpu.SemaphoreType.DMA(()), pltpu.SemaphoreType.DMA(()),
               pltpu.SemaphoreType.DMA((3,)), pltpu.SemaphoreType.DMA((3,))]


class EarlyGram:
    def __init__(self, place, agb, gram, rb, send_r, recv_r, send_x, send_l, send_y, recv):
        self.p, self.agb, self.gram, self.rb = place, agb, gram, rb
        self.send_r, self.recv_r = send_r, recv_r
        self.send_x, self.send_l, self.send_y, self.recv = send_x, send_l, send_y, recv
        p = place
        self.root = p.c == 0
        self.on_x = jnp.logical_and(p.y == 0, p.l == 0)
        self.on_y = p.y == 0

    def scatter(self, d):
        j = row_piece((self.p.r + d) % (NZ * NC))
        return rcopy(self.gram.at[j], self.rb.at[d - 1], self.send_r.at[d - 1], self.recv_r.at[d - 1], self.p.at_row(d))

    def piece(self, send, device):
        part = self.agb.at[pl.ds(GRAM, 2), self.p.piece]
        return rcopy(part, part, send, self.recv, device)

    def to_x(self, d):
        return self.piece(self.send_x.at[d - 1], self.p.at_x(d))

    def to_l(self):
        return self.piece(self.send_l, self.p.at_l())

    def to_y(self, d):
        return self.piece(self.send_y.at[d - 1], self.p.at_y(d))

    def add(self, block, i):
        @pl.when(self.root)
        def _():
            mine = jnp.where(jnp.logical_and(i == 0, self.p.r == 0), 0.0, block)
            prod = dot3(mine.T, mine).reshape(8, SUB, W)
            self.gram[...] = jnp.where(i == 0, prod, self.gram[...] + prod)

    def start(self):
        @pl.when(self.root)
        def _():
            for d in range(1, 8):
                self.scatter(d).start()

    def along_x(self, first):
        @pl.when(self.root)
        def _():
            total = self.gram[self.p.piece]
            for d in range(1, 8):
                self.scatter(d).wait_recv()
                total = total + self.rb[d - 1]
            self.agb[GRAM, self.p.piece] = total
        first.arrive()

        @pl.when(self.root)
        def _():
            for d in (1, 3, 2):
                self.to_x(d).start()

    def along_l(self):
        @pl.when(jnp.logical_and(self.on_x, self.p.x != 0))
        def _():
            self.to_l().wait_recv()

        @pl.when(self.on_x)
        def _():
            self.to_l().start()

    def along_y(self):
        @pl.when(jnp.logical_and(self.on_y, self.p.l != 0))
        def _():
            self.to_l().wait_recv()

        @pl.when(self.on_y)
        def _():
            for d in (4, 3, 5, 2, 6, 1, 7):
                self.to_y(d).start()

    def arrive(self):
        @pl.when(jnp.logical_not(self.on_y))
        def _():
            self.to_l().wait_recv()

    def finish(self):
        @pl.when(self.root)
        def _():
            for d in range(1, 8):
                self.scatter(d).wait_send()
            for d in (1, 2, 3):
                self.to_x(d).wait_send()

        @pl.when(self.on_x)
        def _():
            self.to_l().wait_send()

        @pl.when(self.on_y)
        def _():
            for d in range(1, 8):
                self.to_y(d).wait_send()


EARLY_SEMS = [pltpu.SemaphoreType.DMA((7,)), pltpu.SemaphoreType.DMA((7,)), pltpu.SemaphoreType.DMA((3,)),
              pltpu.SemaphoreType.DMA(()), pltpu.SemaphoreType.DMA((7,)), pltpu.SemaphoreType.DMA(())]


def pivot(t, p0, p1, cols, lane, row, jordan):
    col = cols[0]
    inv = 1.0 / col[t:t + 1, :]
    r0 = jnp.where(lane[t:t + 1] == t, 1.0, p0[t:t + 1]) * inv
    r1 = p1[t:t + 1] * inv
    here = row == t
    apply = jnp.logical_not(here) if jordan else row > t
    factor = jnp.where(apply, col, 0.0)
    rest = []
    for other in cols[1:]:
        ro = other[t:t + 1] * inv
        new = other - factor * ro
        rest.append(jnp.where(here, ro, new) if jordan else new)
    p0 = jnp.where(jnp.logical_and(apply, lane == t), 0.0, p0) - factor * r0
    p1 = p1 - factor * r1
    if jordan:
        p0, p1 = jnp.where(here, r0, p0), jnp.where(here, r1, p1)
    return p0, p1, rest


def group_columns(p0, t):
    return [jnp.broadcast_to(p0[:, u:u + 1], (SUB, 128)) for u in range(t, t + GROUP)]


def turn(v):
    return jnp.concatenate([v[:, SUB:], v[:, :SUB]], axis=1)


def turn_store(ref, body, panel):
    out = turn(body)
    ref[:W - SUB, :] = out[SUB:]
    ref[W - SUB:, :] = turn(panel)


def sweep(j, t_ref, m_ref, row_ref, lt_ref):
    lane = iota((SUB, 128), 1)
    row = iota((SUB, 128), 0)
    lane2 = iota((SUB, W), 1)
    before = row_ref[...]
    m_left = m_ref[:, :128].T[:SUB] + before
    q0 = m_ref[:SUB, :128] + jnp.where(lane < SUB, jnp.concatenate(
        [before[:, :SUB].T, jnp.zeros((SUB, 128 - SUB), F32)], axis=1), 0.0)
    q1 = m_ref[:SUB, 128:]
    p0, p1 = t_ref[:SUB, :128], t_ref[:SUB, 128:]
    for t in range(SUB):
        if t % GROUP == 0:
            p_cols, q_cols = group_columns(p0, t), group_columns(q0, t)
        p0, p1, p_cols = pivot(t, p0, p1, p_cols, lane, row, False)
        q0, q1, q_cols = pivot(t, q0, q1, q_cols, lane, row, True)

    diag = jnp.sum(jnp.where(lane == row, p0, 0.0), axis=1, keepdims=True)
    scale = 1.0 / jnp.sqrt(diag)
    p0, p1 = p0 * scale, p1 * scale
    upper = jnp.where(lane >= row, p0, 0.0)
    inside = jnp.where(lane < row, p0, jnp.where(lane == row, scale, 0.0))
    table = jnp.concatenate([jnp.where(lane < SUB, inside, p0), p1], axis=1)
    live = jnp.logical_and(lane2 < SUB * (8 - j), lane2 >= 0)
    upper = jnp.where(live, jnp.concatenate([upper, p1], axis=1), 0.0)
    first = iota((W, W), 1) < SUB
    t_new = jnp.where(first, 0.0, t_ref[...]) - packed_tdot(jnp.where(lane2 < SUB, 0.0, upper), table)
    panel = jnp.concatenate([q0, q1], axis=1)
    m_new = jnp.where(first, 0.0, m_ref[...]) - packed_tdot(m_left, panel)

    @pl.when(j < 8)
    def _():
        turn_store(t_ref, t_new, table)
        row_ref[...] = upper
        lt_ref[pl.ds(pl.multiple_of(j * SUB, SUB), SUB), :] = pltpu.roll(upper, j * SUB, 1)

    @pl.when(j > 0)
    def _():
        turn_store(m_ref, m_new, panel)


class ColumnSums:
    def __init__(self, place, out, mine, s1, s2, s3, rows, rb1, rb2, rb3, c1, c2, c3, c4, gather):
        self.p, self.out, self.mine, self.rows = place, out, mine, rows
        self.s1, self.s2, self.s3 = s1, s2, s3
        self.rb1, self.rb2, self.rb3 = rb1, rb2, rb3
        self.c1, self.c2, self.c3, self.c4 = c1, c2, c3, c4
        self.gather = RowGather(place, out, 0, 3, *gather)
        self.here = pl.ds(pl.multiple_of(place.x * 8, 8), 8)

    def to_l(self):
        return rcopy(self.mine, self.rb1, self.c1.at[0], self.c1.at[1], self.p.at_l())

    def to_x(self, d):
        x = (self.p.x + d) % NX
        part = self.s1.at[:, pl.ds(pl.multiple_of(x * 8, 8), 8)]
        return rcopy(part, self.rb2.at[d - 1], self.c2.at[0, d - 1], self.c2.at[1, d - 1], self.p.at_x(d))

    def to_y(self, d):
        return rcopy(self.s2, self.rb3.at[d - 1], self.c3.at[0, d - 1], self.c3.at[1, d - 1], self.p.at_y(d))

    def back_x(self, d):
        part = self.rows.at[:, self.here]
        return rcopy(self.s3, part, self.c4.at[0, d - 1], self.c4.at[1, d - 1], self.p.at_x(d))

    def along_l(self):
        self.to_l().start()

    def along_x(self):
        self.to_l().wait_recv()
        self.s1[...] = self.mine[...] + self.rb1[...]
        for d in (1, 3, 2):
            self.to_x(d).start()

    def along_y(self):
        total = self.s1[:, self.here]
        for d in (1, 2, 3):
            self.to_x(d).wait_recv()
            total = total + self.rb2[d - 1]
        self.s2[...] = total
        for d in (4, 3, 5, 2, 6, 1, 7):
            self.to_y(d).start()

    def return_x(self):
        total = self.s2[...]
        for d in range(1, 8):
            self.to_y(d).wait_recv()
            total = total + self.rb3[d - 1]
        self.s3[...] = total
        self.rows[:, self.here] = total
        for d in (1, 3, 2):
            self.back_x(d).start()

    def along_row(self):
        for d in (1, 2, 3):
            self.back_x(d).wait_recv()
        self.out[:, self.p.piece] = self.rows[...]
        self.gather.start()

    def finish(self):
        self.to_l().wait_send()
        for d in (1, 2, 3):
            self.to_x(d).wait_send()
            self.back_x(d).wait_send()
        for d in range(1, 8):
            self.to_y(d).wait_send()


SUM_BUFS = [pltpu.VMEM((3, 8, SUB, W), F32), pltpu.VMEM((3, SUB, W), F32), pltpu.VMEM((3, SUB, W), F32),
            pltpu.VMEM((3, 8, W), F32), pltpu.VMEM((3, 8, W), F32), pltpu.VMEM((3, SUB, W), F32),
            pltpu.VMEM((3, SUB, W), F32), pltpu.VMEM((3, 3, 8, W), F32), pltpu.VMEM((7, 3, 8, W), F32)]
SUM_SEMS = [pltpu.SemaphoreType.DMA((2,)), pltpu.SemaphoreType.DMA((2, 3)),
            pltpu.SemaphoreType.DMA((2, 7)), pltpu.SemaphoreType.DMA((2, 3))]


class Sems:
    def __init__(self, refs):
        self.refs, self.at = refs, 0

    def take(self, group):
        self.at += len(group)
        return self.refs[self.at - len(group):self.at]


def panel_kernel(a_hbm, out, a_ref, prow, irow, lt, y_ref, k_ref, it_ref, r_ref, s_ref, u_ref, agb, src, near_src, gram, gram_rb, m, row, part, rb_core, sums, rb_z, load, store, *refs):
    sems = Sems(refs)
    sum_bufs = sems.take(SUM_BUFS)
    p = Place()

    def fetch(i):
        return pltpu.make_async_copy(a_hbm.at[i], a_ref.at[i], load.at[i])

    loop(NY, lambda i: fetch(i).start())
    greet([p.at_row(d) for d in range(1, 8)] + [p.at_y(d) for d in range(1, 8)] + [p.at_l()]
          + [p.at_x(d) for d in (1, 2, 3)])
    fetch(0).wait()

    spread_sems = sems.take(SPREAD_SEMS)
    spread = Spread(p, prow, *spread_sems)
    home_row = p.x * NC + p.l
    home = jnp.logical_and(p.diag, p.r == 0)

    @pl.when(p.r == 0)
    def _():
        src[...] = jnp.where(p.c == 0, 0.0, a_ref[0])

    @pl.when(p.r == 1)
    def _():
        src[...] = a_ref[0]

    home_sem = sems.take([0])[0]

    def to_home(q):
        rows = pl.ds(pl.multiple_of(q * QR, QR), QR)
        return rcopy(src.at[rows], prow.at[p.y, rows], home_sem.at[q], spread_sems[0].at[p.y, q], (home_row, p.c))

    @pl.when(home)
    def _():
        prow[p.y] = src[...]

    sends_home = jnp.logical_and(p.r == 0, home_row != 0)

    @pl.when(sends_home)
    def _():
        loop(NQ, lambda q: to_home(q).start())

    panel = RowScatter(p, 0, p.c >= 0, src, agb.at[PANEL], *sems.take(SCATTER_SEMS))
    following = RowScatter(p, 1, p.c >= 0, src, agb.at[NEXT], *sems.take(SCATTER_SEMS))
    first = RowScatter(p, 1, p.c == 0, near_src, agb.at[FIRST], *sems.take(SCATTER_SEMS))
    early = EarlyGram(p, agb, gram, gram_rb, *sems.take(EARLY_SEMS))
    columns = RowGather(p, agb, PANEL, NEXT + 1, *sems.take(GATHER_SEMS))
    grams = RowGather(p, agb, GRAM, GRAM + 1, *sems.take(GATHER_SEMS))
    firsts = RowGather(p, agb, FIRST, FIRST + 1, *sems.take(GATHER_SEMS))
    prods = RowGather(p, agb, PROD, PROD + 1, *sems.take(GATHER_SEMS))
    reduce = RowReduce(p, part, rb_core, sums, rb_z, *sems.take(REDUCE_SEMS))

    panel.start()
    following.start()
    loop(NY - 1, lambda i: fetch(i + 1).wait())

    @pl.when(jnp.logical_and(p.r == 1, p.c == 0))
    def _():
        near_src[...] = a_ref[0].T

    first.start()

    def product(i, half):
        rows = pl.ds(half * (W // 2), W // 2)
        part[half * NZ:(half + 1) * NZ] += dot3(prow[i, rows], a_ref[i]).reshape(NZ, SUB, W)

    def products(*offsets):
        for d in offsets:
            product((p.y + d) % NY, 0)

        @pl.when(p.native)
        def _():
            for d in offsets:
                product((p.y + d) % NY, 1)

    part[...] = jnp.zeros_like(part)
    spread.own(home, lambda q: early.add(a_ref[q], q))
    early.start()
    panel.arrive()
    following.arrive()
    columns.start()
    spread.ring(1)
    early.along_x(first)
    products(0)
    spread.ring(2)
    early.along_l()
    columns.relay()
    products(1, 7)
    spread.ring(3)
    early.along_y()
    spread.last()
    products(2, 6)
    early.arrive()
    grams.start()
    firsts.start()
    products(3, 5, 4)

    @pl.when(jnp.logical_not(p.native))
    def _():
        def rest(t):
            i = (p.y + t) % NY
            spread.late(i)
            product(i, 1)

        loop(NY, rest)

    reduce.start()
    columns.finish()
    grams.relay()
    reduce.across()
    grams.finish()
    firsts.relay()

    y_ref[...] = agb[GRAM].reshape(W, W)
    row[...] = jnp.zeros_like(row)
    colsum = ColumnSums(p, *sum_bufs, *sems.take(SUM_SEMS), sems.take(GATHER_SEMS))
    images = Spread(p, irow, *sems.take(SPREAD_SEMS))

    def step(j):
        sweep(j, y_ref, m, row, lt)

        @pl.when(j == 0)
        def _():
            firsts.finish()
            m[...] = -agb[FIRST].reshape(W, W)

        @pl.when(j == 1)
        def _():
            total = reduce.total()
            agb[PROD, p.piece] = total
            prods.start()
            colsum.mine[0] = dot6(total, agb[PANEL].reshape(W, W), NT)
            colsum.mine[1] = jnp.where(p.c == 1, total, 0.0)
            colsum.mine[2] = jnp.where(p.c == 1, agb[NEXT, p.piece], 0.0)
            colsum.along_l()

        @pl.when(j == 3)
        def _():
            colsum.along_x()

        @pl.when(j == 4)
        def _():
            prods.relay()

        @pl.when(j == 5)
        def _():
            colsum.along_y()

        @pl.when(j == 8)
        def _():
            colsum.return_x()

    loop(9, step)
    prods.finish()

    it_ref[...] = agb[NEXT].reshape(W, W) - dot6(y_ref[...], agb[PROD].reshape(W, W))

    @pl.when(p.diag)
    def _():
        irow[p.y] = it_ref[...].T
        images.own(p.diag)

    colsum.along_row()
    shifted = jnp.where(p.c == 1, lt[...].T, 0.0) - agb[PANEL].reshape(W, W)
    r_ref[...] = dot6(m[...], shifted)

    @pl.when(jnp.logical_not(p.diag))
    def _():
        images.own(p.diag)

    k_ref[...] = dot6(m[...], lt[...], NT)

    def away(i, half):
        rows = pl.ds(half * (W // 2), W // 2)
        a_ref[i, rows] -= dot3(irow[i, rows], r_ref[...])

    def aways(*offsets):
        for d in offsets:
            away((p.y + d) % NY, 0)

        @pl.when(p.native)
        def _():
            for d in offsets:
                away((p.y + d) % NY, 1)

    def flip(i):
        prow[i] = prow[i].T

    spread.drain()
    images.ring(1)
    reduce.finish()
    early.finish()
    for each in (panel, following, first):
        each.finish()

    @pl.when(sends_home)
    def _():
        loop(NQ, lambda q: to_home(q).wait_send())

    loop(4, flip)
    aways(0)
    images.ring(2)
    colsum.gather.relay()
    loop(4, lambda i: flip(4 + i))
    aways(1, 7)
    images.ring(3)
    images.last()
    aways(2, 6, 3, 5, 4)
    colsum.gather.finish()
    inv = y_ref[...]
    far = dot3(inv, r_ref[...], TN)
    prod = colsum.out[1].reshape(W, W)
    bent = dot3(inv, dot3(colsum.out[0].reshape(W, W), far) - dot3(prod, r_ref[...]))
    bent = bent + (dot3(colsum.out[2].reshape(W, W), r_ref[...]) - dot3(prod, far, TN))
    s_ref[...] = dot3(k_ref[...], it_ref[...] - bent, TN)
    u_ref[...] = dot3(inv, s_ref[...], TN)

    def put(i):
        return pltpu.make_async_copy(a_ref.at[i], out.at[i], store.at[i])

    def update(t):
        i = (p.y + t) % NY
        images.late(i)

        @pl.when(jnp.logical_not(p.native))
        def _():
            away(i, 1)

        b = i * (NZ * NC) + p.r
        old = a_ref[i]
        new = old + dot3(prow[i], u_ref[...])
        a_ref[i] = jnp.where(b == 1, new - s_ref[...], new)

        @pl.when(p.c == 0)
        def _():
            a_ref[i] = jnp.where(b == 0, old, jnp.where(b == 1, lt[...], 0.0))

        @pl.when(jnp.logical_and(p.c > 0, b == 0))
        def _():
            a_ref[i] = jnp.where(p.c == 1, lt[...].T, 0.0)

        put(i).start()

    loop(NY, update)
    colsum.finish()
    images.drain()
    loop(NY, lambda i: put(i).wait())


def panel_call(slab):
    dma = pltpu.SemaphoreType.DMA
    square = pltpu.VMEM((W, W), F32)
    blocks = pltpu.VMEM((NY, W, W), F32)
    return pl.pallas_call(
        panel_kernel,
        out_shape=jax.ShapeDtypeStruct((NY, W, W), F32),
        in_specs=[pl.BlockSpec(memory_space=pltpu.HBM)],
        out_specs=pl.BlockSpec(memory_space=pl.ANY),
        scratch_shapes=[blocks] * 3 + [square] * 7 + [
            pltpu.VMEM((5, 8, SUB, W), F32),
            square,
            square,
            pltpu.VMEM((8, SUB, W), F32),
            pltpu.VMEM((7, SUB, W), F32),
            square,
            pltpu.VMEM((SUB, W), F32),
        ] + REDUCE_BUFS + [dma((NY,)), dma((NY,))] + SUM_BUFS
        + SPREAD_SEMS + [dma((NQ,))] + SCATTER_SEMS * 3 + EARLY_SEMS + GATHER_SEMS * 4 + REDUCE_SEMS
        + SUM_SEMS + GATHER_SEMS + SPREAD_SEMS,
        compiler_params=pltpu.CompilerParams(
            collective_id=0, has_side_effects=True, vmem_limit_bytes=VMEM_LIMIT),
        name="panel_step",
    )(slab)


def on_device(matrix):
    slab = matrix.reshape(NY, W, W)
    return panel_call(slab).reshape(matrix.shape)


def solution(mesh):
    return jax.shard_map(
        on_device,
        mesh=mesh,
        in_specs=(P(None, "row", None, "col"),),
        out_specs=P(None, "row", None, "col"),
        check_vma=False,
    )
```

```python
import functools

import jax
import jax.numpy as jnp
from jax import lax
from jax.experimental import pallas as pl
from jax.experimental.pallas import tpu as pltpu
from jax.sharding import PartitionSpec as P

NY, NX, NZ, NL, NC = 8, 4, 4, 2, 2
W = 256
SUB = 32
NQ = 8
QR = W // NQ
GROUP = 8
F32, BF16 = jnp.float32, jnp.bfloat16
MESH = pl.DeviceIdType.MESH
VMEM_LIMIT = 50 * 1024 * 1024
NN = (((1,), (0,)), ((), ()))
NT = (((1,), (1,)), ((), ()))
TN = (((0,), (0,)), ((), ()))


def split2(v):
    hi = v.astype(BF16)
    return hi, (v - hi.astype(F32)).astype(BF16)


def split3(v):
    a = v.astype(BF16)
    rest = v - a.astype(F32)
    b = rest.astype(BF16)
    return a, b, (rest - b.astype(F32)).astype(BF16)


def mm(a, b, dims):
    return lax.dot_general(a, b, dims, preferred_element_type=F32)


def dot3(a, b, dims=NN):
    ah, al = split2(a)
    bh, bl = split2(b)
    return mm(ah, bh, dims) + (mm(ah, bl, dims) + mm(al, bh, dims))


def dot6(a, b, dims=NN):
    a1, a2, a3 = split3(a)
    b1, b2, b3 = split3(b)
    low = mm(a2, b2, dims) + (mm(a1, b3, dims) + mm(a3, b1, dims))
    return mm(a1, b1, dims) + ((mm(a1, b2, dims) + mm(a2, b1, dims)) + low)


def packed_tdot(a, b):
    a1, a2, a3 = split3(a)
    b1, b2, b3 = split3(b)
    left = jnp.concatenate([a1, a1, a2, a2, a1, a3], axis=0)
    right = jnp.concatenate([b1, b2, b1, b2, b3, b1], axis=0)
    return mm(left, right, TN)


def iota(shape, dim):
    return lax.broadcasted_iota(jnp.int32, shape, dim)


class Place:
    def __init__(self):
        self.r = lax.axis_index("row")
        self.c = lax.axis_index("col")
        self.z, self.h = self.r // NC, self.r % NC
        self.y, self.x, self.l = self.c // (NX * NL), (self.c // NL) % NX, self.c % NL
        self.piece = self.h * NZ + self.z
        self.native = self.l == self.h
        self.diag = jnp.logical_and(self.native, self.x == self.z)

    def at_y(self, d):
        return (self.r, ((self.y + d) % NY * NX + self.x) * NL + self.l)

    def at_x(self, d):
        return (self.r, (self.y * NX + (self.x + d) % NX) * NL + self.l)

    def at_l(self):
        return (self.r, (self.y * NX + self.x) * NL + (1 - self.l))

    def at_z(self, d):
        return (((self.z + d) % NZ) * NC + self.h, self.c)

    def at_core(self):
        return (self.z * NC + (1 - self.h), self.c)

    def at_row(self, d):
        return ((self.r + d) % (NZ * NC), self.c)


def rcopy(src, dst, send, recv, device):
    return pltpu.make_async_remote_copy(
        src_ref=src, dst_ref=dst, send_sem=send, recv_sem=recv, device_id=device, device_id_type=MESH
    )


def greet(devices):
    barrier = pltpu.get_barrier_semaphore()
    for device in devices:
        pl.semaphore_signal(barrier, inc=1, device_id=device, device_id_type=MESH)
    pl.semaphore_wait(barrier, len(devices))


def loop(n, body):
    def step(t, carry):
        body(t)
        return carry

    lax.fori_loop(0, n, step, 0)


class Spread:
    def __init__(self, place, buf, recv, send_x, send_y, send_l):
        self.p, self.buf, self.recv = place, buf, recv
        self.send_x, self.send_y, self.send_l = send_x, send_y, send_l

    def chunk(self, i, q):
        return self.buf.at[i, pl.ds(pl.multiple_of(q * QR, QR), QR)]

    def copy(self, i, q, send, device):
        part = self.chunk(i, q)
        return rcopy(part, part, send, self.recv.at[i, q], device)

    def to_x(self, d, q):
        return self.copy(self.p.y, q, self.send_x.at[d - 1], self.p.at_x(d))

    def to_y(self, side, s, q):
        sign = 1 if side == 0 else -1
        i = (self.p.y - sign * s + NY) % NY
        return self.copy(i, q, self.send_y.at[side, s], self.p.at_y(sign + NY))

    def to_l(self, i, q):
        return self.copy(i, q, self.send_l.at[i], self.p.at_l())

    def arrive(self, i, q):
        self.copy(i, q, self.send_l.at[i], self.p.at_l()).wait_recv()

    def own(self, home, beside=lambda q: None):
        p = self.p

        def body(q):
            @pl.when(jnp.logical_and(p.native, jnp.logical_not(home)))
            def _():
                self.arrive(p.y, q)

            @pl.when(jnp.logical_and(jnp.logical_not(p.native), q < NQ // 2))
            def _():
                self.arrive(p.y, q)

            @pl.when(p.diag)
            def _():
                for d in (1, 3, 2):
                    self.to_x(d, q).start()

            @pl.when(p.native)
            def _():
                self.to_l(p.y, q).start()

            @pl.when(jnp.logical_or(p.native, q < NQ // 2))
            def _():
                self.to_y(0, 0, q).start()
                self.to_y(1, 0, q).start()

            beside(q)

        loop(NQ, body)

    def sends_y(self, side, s, q):
        if s < 3:
            return jnp.logical_or(self.p.native, q < NQ // 2)
        if side == 0:
            return q < jnp.where(self.p.native, NQ // 2, NQ // 4)
        return jnp.where(self.p.native, q, (q % (NQ // 2)) * 2 * (q < NQ // 2)) >= NQ // 2

    def ring(self, s):
        p = self.p

        def body(q):
            for side in (0, 1):
                sign = 1 if side == 0 else -1
                i = (p.y - sign * s + NY) % NY

                @pl.when(jnp.logical_or(p.native, q < NQ // 2))
                def _(i=i):
                    self.arrive(i, q)

                @pl.when(self.sends_y(side, s, q))
                def _(side=side):
                    self.to_y(side, s, q).start()

                @pl.when(jnp.logical_and(p.native, q >= NQ // 2))
                def _(i=i):
                    self.to_l(i, q).start()

        loop(NQ, body)

    def last(self):
        p = self.p
        i = (p.y + 4) % NY

        def body(q):
            @pl.when(jnp.logical_or(p.native, q < NQ // 2))
            def _():
                self.arrive(i, q)

            @pl.when(jnp.logical_and(p.native, q >= NQ // 2))
            def _():
                self.to_l(i, q).start()

        loop(NQ, body)

    def late(self, i):
        @pl.when(jnp.logical_not(self.p.native))
        def _():
            loop(NQ // 2, lambda q: self.arrive(i, NQ // 2 + q))

    def sent(self, rows, send):
        part = self.buf.at[self.p.y, pl.ds(0, rows)]
        rcopy(part, part, send, self.recv.at[0, 0], self.p.at_l()).wait_send()

    def drain(self):
        p = self.p

        @pl.when(p.diag)
        def _():
            for d in range(3):
                self.sent(W, self.send_x.at[d])

        def ring(full):
            for side in (0, 1):
                for s in range(3):
                    self.sent(full, self.send_y.at[side, s])
                self.sent(full // 2, self.send_y.at[side, 3])

        @pl.when(p.native)
        def _():
            ring(W)
            self.sent(W, self.send_l.at[p.y])
            loop(NY - 1, lambda t: self.sent(W // 2, self.send_l.at[(p.y + 1 + t) % NY]))

        @pl.when(jnp.logical_not(p.native))
        def _():
            ring(W // 2)


SPREAD_SEMS = [
    pltpu.SemaphoreType.DMA((NY, NQ)),
    pltpu.SemaphoreType.DMA((3,)),
    pltpu.SemaphoreType.DMA((2, 4)),
    pltpu.SemaphoreType.DMA((NY,)),
]


class RowGather:
    def __init__(self, place, buf, lo, hi, recv, send):
        self.p, self.buf, self.lo, self.hi = place, buf, lo, hi
        self.recv, self.send = recv, send

    def copy(self, j, slot, device):
        part = self.buf.at[pl.ds(self.lo, self.hi - self.lo), j]
        return rcopy(part, part, self.send.at[slot], self.recv.at[j], device)

    def to_z(self, d):
        return self.copy(self.p.piece, d - 1, self.p.at_z(d))

    def to_core(self, d):
        j = self.p.h * NZ + (self.p.z - d + NZ) % NZ
        return self.copy(j, 3 + d, self.p.at_core())

    def start(self):
        for d in (1, 3, 2):
            self.to_z(d).start()
        self.to_core(0).start()

    def relay(self):
        for d in (1, 3, 2):
            self.to_core(d).wait_recv()
            self.to_core(d).start()

    def finish(self):
        for d in range(4):
            j = (1 - self.p.h) * NZ + (self.p.z - d + NZ) % NZ
            self.copy(j, 3 + d, self.p.at_core()).wait_recv()
        for d in (1, 2, 3):
            self.to_z(d).wait_send()
        for d in range(4):
            self.to_core(d).wait_send()


GATHER_SEMS = [pltpu.SemaphoreType.DMA((NZ * NC,)), pltpu.SemaphoreType.DMA((7,))]


def row_piece(r):
    return (r % NC) * NZ + r // NC


class RowScatter:
    def __init__(self, place, root, active, src, dst, recv, send):
        self.p, self.src, self.dst = place, src, dst
        self.recv, self.send = recv, send
        self.is_root = jnp.logical_and(place.r == root, active)
        self.is_leaf = jnp.logical_and(place.r != root, active)

    def copy(self, d):
        j = row_piece((self.p.r + d) % (NZ * NC))
        part = self.src.at[pl.ds(pl.multiple_of(j * SUB, SUB), SUB)]
        return rcopy(part, self.dst.at[j], self.send.at[d - 1], self.recv, self.p.at_row(d))

    def start(self):
        @pl.when(self.is_root)
        def _():
            for d in range(1, 8):
                self.copy(d).start()
            self.dst[self.p.piece] = self.src[pl.ds(pl.multiple_of(self.p.piece * SUB, SUB), SUB)]

    def arrive(self):
        @pl.when(self.is_leaf)
        def _():
            self.copy(1).wait_recv()

    def finish(self):
        @pl.when(self.is_root)
        def _():
            for d in range(1, 8):
                self.copy(d).wait_send()


SCATTER_SEMS = [pltpu.SemaphoreType.DMA(()), pltpu.SemaphoreType.DMA((7,))]

GRAM, FIRST, PROD, PANEL, NEXT = range(5)


class RowReduce:
    def __init__(self, place, part, rb_core, sums, rb_z, send_c, recv_c, send_z, recv_z):
        self.p, self.part, self.rb_core, self.sums, self.rb_z = place, part, rb_core, sums, rb_z
        self.send_z, self.recv_z = send_z, recv_z
        other = pl.ds(pl.multiple_of((1 - place.h) * NZ, NZ), NZ)
        self.out = rcopy(part.at[other], rb_core, send_c, recv_c, place.at_core())

    def to_z(self, d):
        p = self.p
        return rcopy(self.sums.at[(p.z + d) % NZ], self.rb_z.at[d - 1],
                     self.send_z.at[d - 1], self.recv_z.at[d - 1], p.at_z(d))

    def start(self):
        self.out.start()

    def across(self):
        self.out.wait_recv()
        mine = pl.ds(pl.multiple_of(self.p.h * NZ, NZ), NZ)
        self.sums[...] = self.part[mine] + self.rb_core[...]
        for d in (1, 3, 2):
            self.to_z(d).start()

    def total(self):
        total = self.sums[self.p.z]
        for d in (1, 3, 2):
            self.to_z(d).wait_recv()
            total = total + self.rb_z[d - 1]
        return total

    def finish(self):
        self.out.wait_send()
        for d in (1, 2, 3):
            self.to_z(d).wait_send()


REDUCE_BUFS = [
    pltpu.VMEM((8, SUB, W), F32),
    pltpu.VMEM((NZ, SUB, W), F32),
    pltpu.VMEM((NZ, SUB, W), F32),
    pltpu.VMEM((3, SUB, W), F32),
]
REDUCE_SEMS = [pltpu.SemaphoreType.DMA(()), pltpu.SemaphoreType.DMA(()),
               pltpu.SemaphoreType.DMA((3,)), pltpu.SemaphoreType.DMA((3,))]


class EarlyGram:
    def __init__(self, place, agb, gram, rb, send_r, recv_r, send_x, send_l, send_y, recv):
        self.p, self.agb, self.gram, self.rb = place, agb, gram, rb
        self.send_r, self.recv_r = send_r, recv_r
        self.send_x, self.send_l, self.send_y, self.recv = send_x, send_l, send_y, recv
        p = place
        self.root = p.c == 0
        self.on_x = jnp.logical_and(p.y == 0, p.l == 0)
        self.on_y = p.y == 0

    def scatter(self, d):
        j = row_piece((self.p.r + d) % (NZ * NC))
        return rcopy(self.gram.at[j], self.rb.at[d - 1], self.send_r.at[d - 1], self.recv_r.at[d - 1], self.p.at_row(d))

    def piece(self, send, device):
        part = self.agb.at[pl.ds(GRAM, 2), self.p.piece]
        return rcopy(part, part, send, self.recv, device)

    def to_x(self, d):
        return self.piece(self.send_x.at[d - 1], self.p.at_x(d))

    def to_l(self):
        return self.piece(self.send_l, self.p.at_l())

    def to_y(self, d):
        return self.piece(self.send_y.at[d - 1], self.p.at_y(d))

    def add(self, block, i):
        @pl.when(self.root)
        def _():
            mine = jnp.where(jnp.logical_and(i == 0, self.p.r == 0), 0.0, block)
            prod = dot3(mine.T, mine).reshape(8, SUB, W)
            self.gram[...] = jnp.where(i == 0, prod, self.gram[...] + prod)

    def start(self):
        @pl.when(self.root)
        def _():
            for d in range(1, 8):
                self.scatter(d).start()

    def along_x(self, first):
        @pl.when(self.root)
        def _():
            total = self.gram[self.p.piece]
            for d in range(1, 8):
                self.scatter(d).wait_recv()
                total = total + self.rb[d - 1]
            self.agb[GRAM, self.p.piece] = total
        first.arrive()

        @pl.when(self.root)
        def _():
            for d in (1, 3, 2):
                self.to_x(d).start()

    def along_l(self):
        @pl.when(jnp.logical_and(self.on_x, self.p.x != 0))
        def _():
            self.to_l().wait_recv()

        @pl.when(self.on_x)
        def _():
            self.to_l().start()

    def along_y(self):
        @pl.when(jnp.logical_and(self.on_y, self.p.l != 0))
        def _():
            self.to_l().wait_recv()

        @pl.when(self.on_y)
        def _():
            for d in (4, 3, 5, 2, 6, 1, 7):
                self.to_y(d).start()

    def arrive(self):
        @pl.when(jnp.logical_not(self.on_y))
        def _():
            self.to_l().wait_recv()

    def finish(self):
        @pl.when(self.root)
        def _():
            for d in range(1, 8):
                self.scatter(d).wait_send()
            for d in (1, 2, 3):
                self.to_x(d).wait_send()

        @pl.when(self.on_x)
        def _():
            self.to_l().wait_send()

        @pl.when(self.on_y)
        def _():
            for d in range(1, 8):
                self.to_y(d).wait_send()


EARLY_SEMS = [pltpu.SemaphoreType.DMA((7,)), pltpu.SemaphoreType.DMA((7,)), pltpu.SemaphoreType.DMA((3,)),
              pltpu.SemaphoreType.DMA(()), pltpu.SemaphoreType.DMA((7,)), pltpu.SemaphoreType.DMA(())]


def pivot(t, p0, p1, cols, lane, row, jordan):
    col = cols[0]
    inv = 1.0 / col[t:t + 1, :]
    r0 = jnp.where(lane[t:t + 1] == t, 1.0, p0[t:t + 1]) * inv
    r1 = p1[t:t + 1] * inv
    here = row == t
    apply = jnp.logical_not(here) if jordan else row > t
    factor = jnp.where(apply, col, 0.0)
    rest = []
    for other in cols[1:]:
        ro = other[t:t + 1] * inv
        new = other - factor * ro
        rest.append(jnp.where(here, ro, new) if jordan else new)
    p0 = jnp.where(jnp.logical_and(apply, lane == t), 0.0, p0) - factor * r0
    p1 = p1 - factor * r1
    if jordan:
        p0, p1 = jnp.where(here, r0, p0), jnp.where(here, r1, p1)
    return p0, p1, rest


def group_columns(p0, t):
    return [jnp.broadcast_to(p0[:, u:u + 1], (SUB, 128)) for u in range(t, t + GROUP)]


def turn(v):
    return jnp.concatenate([v[:, SUB:], v[:, :SUB]], axis=1)


def turn_store(ref, body, panel):
    out = turn(body)
    ref[:W - SUB, :] = out[SUB:]
    ref[W - SUB:, :] = turn(panel)


def sweep(j, t_ref, m_ref, row_ref, lt_ref):
    lane = iota((SUB, 128), 1)
    row = iota((SUB, 128), 0)
    lane2 = iota((SUB, W), 1)
    before = row_ref[...]
    m_left = m_ref[:, :128].T[:SUB] + before
    q0 = m_ref[:SUB, :128] + jnp.where(lane < SUB, jnp.concatenate(
        [before[:, :SUB].T, jnp.zeros((SUB, 128 - SUB), F32)], axis=1), 0.0)
    q1 = m_ref[:SUB, 128:]
    p0, p1 = t_ref[:SUB, :128], t_ref[:SUB, 128:]
    for t in range(SUB):
        if t % GROUP == 0:
            p_cols, q_cols = group_columns(p0, t), group_columns(q0, t)
        p0, p1, p_cols = pivot(t, p0, p1, p_cols, lane, row, False)
        q0, q1, q_cols = pivot(t, q0, q1, q_cols, lane, row, True)

    diag = jnp.sum(jnp.where(lane == row, p0, 0.0), axis=1, keepdims=True)
    scale = 1.0 / jnp.sqrt(diag)
    p0, p1 = p0 * scale, p1 * scale
    upper = jnp.where(lane >= row, p0, 0.0)
    inside = jnp.where(lane < row, p0, jnp.where(lane == row, scale, 0.0))
    table = jnp.concatenate([jnp.where(lane < SUB, inside, p0), p1], axis=1)
    live = jnp.logical_and(lane2 < SUB * (8 - j), lane2 >= 0)
    upper = jnp.where(live, jnp.concatenate([upper, p1], axis=1), 0.0)
    first = iota((W, W), 1) < SUB
    t_new = jnp.where(first, 0.0, t_ref[...]) - packed_tdot(jnp.where(lane2 < SUB, 0.0, upper), table)
    panel = jnp.concatenate([q0, q1], axis=1)
    m_new = jnp.where(first, 0.0, m_ref[...]) - packed_tdot(m_left, panel)

    @pl.when(j < 8)
    def _():
        turn_store(t_ref, t_new, table)
        row_ref[...] = upper
        lt_ref[pl.ds(pl.multiple_of(j * SUB, SUB), SUB), :] = pltpu.roll(upper, j * SUB, 1)

    @pl.when(j > 0)
    def _():
        turn_store(m_ref, m_new, panel)


class ColumnSums:
    def __init__(self, place, out, mine, s1, s2, s3, rows, rb1, rb2, rb3, c1, c2, c3, c4, gather):
        self.p, self.out, self.mine, self.rows = place, out, mine, rows
        self.s1, self.s2, self.s3 = s1, s2, s3
        self.rb1, self.rb2, self.rb3 = rb1, rb2, rb3
        self.c1, self.c2, self.c3, self.c4 = c1, c2, c3, c4
        self.gather = RowGather(place, out, 0, 3, *gather)
        self.here = pl.ds(pl.multiple_of(place.x * 8, 8), 8)

    def to_l(self):
        return rcopy(self.mine, self.rb1, self.c1.at[0], self.c1.at[1], self.p.at_l())

    def to_x(self, d):
        x = (self.p.x + d) % NX
        part = self.s1.at[:, pl.ds(pl.multiple_of(x * 8, 8), 8)]
        return rcopy(part, self.rb2.at[d - 1], self.c2.at[0, d - 1], self.c2.at[1, d - 1], self.p.at_x(d))

    def to_y(self, d):
        return rcopy(self.s2, self.rb3.at[d - 1], self.c3.at[0, d - 1], self.c3.at[1, d - 1], self.p.at_y(d))

    def back_x(self, d):
        part = self.rows.at[:, self.here]
        return rcopy(self.s3, part, self.c4.at[0, d - 1], self.c4.at[1, d - 1], self.p.at_x(d))

    def along_l(self):
        self.to_l().start()

    def along_x(self):
        self.to_l().wait_recv()
        self.s1[...] = self.mine[...] + self.rb1[...]
        for d in (1, 3, 2):
            self.to_x(d).start()

    def along_y(self):
        total = self.s1[:, self.here]
        for d in (1, 2, 3):
            self.to_x(d).wait_recv()
            total = total + self.rb2[d - 1]
        self.s2[...] = total
        for d in (4, 3, 5, 2, 6, 1, 7):
            self.to_y(d).start()

    def return_x(self):
        total = self.s2[...]
        for d in range(1, 8):
            self.to_y(d).wait_recv()
            total = total + self.rb3[d - 1]
        self.s3[...] = total
        self.rows[:, self.here] = total
        for d in (1, 3, 2):
            self.back_x(d).start()

    def along_row(self):
        for d in (1, 2, 3):
            self.back_x(d).wait_recv()
        self.out[:, self.p.piece] = self.rows[...]
        self.gather.start()

    def finish(self):
        self.to_l().wait_send()
        for d in (1, 2, 3):
            self.to_x(d).wait_send()
            self.back_x(d).wait_send()
        for d in range(1, 8):
            self.to_y(d).wait_send()


SUM_BUFS = [pltpu.VMEM((3, 8, SUB, W), F32), pltpu.VMEM((3, SUB, W), F32), pltpu.VMEM((3, SUB, W), F32),
            pltpu.VMEM((3, 8, W), F32), pltpu.VMEM((3, 8, W), F32), pltpu.VMEM((3, SUB, W), F32),
            pltpu.VMEM((3, SUB, W), F32), pltpu.VMEM((3, 3, 8, W), F32), pltpu.VMEM((7, 3, 8, W), F32)]
SUM_SEMS = [pltpu.SemaphoreType.DMA((2,)), pltpu.SemaphoreType.DMA((2, 3)),
            pltpu.SemaphoreType.DMA((2, 7)), pltpu.SemaphoreType.DMA((2, 3))]


class Sems:
    def __init__(self, refs):
        self.refs, self.at = refs, 0

    def take(self, group):
        self.at += len(group)
        return self.refs[self.at - len(group):self.at]


def panel_kernel(a_hbm, out, a_ref, prow, irow, lt, y_ref, k_ref, it_ref, r_ref, s_ref, u_ref, agb, src, near_src, gram, gram_rb, m, row, part, rb_core, sums, rb_z, load, *refs):
    sems = Sems(refs)
    sum_bufs = sems.take(SUM_BUFS)
    p = Place()

    def fetch(i):
        return pltpu.make_async_copy(a_hbm.at[i], a_ref.at[i], load.at[i])

    loop(NY, lambda i: fetch(i).start())
    greet([p.at_row(d) for d in range(1, 8)] + [p.at_y(d) for d in range(1, 8)] + [p.at_l()]
          + [p.at_x(d) for d in (1, 2, 3)])
    fetch(0).wait()

    spread_sems = sems.take(SPREAD_SEMS)
    spread = Spread(p, prow, *spread_sems)
    home_row = p.x * NC + p.l
    home = jnp.logical_and(p.diag, p.r == 0)

    @pl.when(p.r == 0)
    def _():
        src[...] = jnp.where(p.c == 0, 0.0, a_ref[0])

    @pl.when(p.r == 1)
    def _():
        src[...] = a_ref[0]

    home_sem = sems.take([0])[0]

    def to_home(q):
        rows = pl.ds(pl.multiple_of(q * QR, QR), QR)
        return rcopy(src.at[rows], prow.at[p.y, rows], home_sem.at[q], spread_sems[0].at[p.y, q], (home_row, p.c))

    @pl.when(home)
    def _():
        prow[p.y] = src[...]

    sends_home = jnp.logical_and(p.r == 0, home_row != 0)

    @pl.when(sends_home)
    def _():
        loop(NQ, lambda q: to_home(q).start())

    panel = RowScatter(p, 0, p.c >= 0, src, agb.at[PANEL], *sems.take(SCATTER_SEMS))
    following = RowScatter(p, 1, p.c >= 0, src, agb.at[NEXT], *sems.take(SCATTER_SEMS))
    first = RowScatter(p, 1, p.c == 0, near_src, agb.at[FIRST], *sems.take(SCATTER_SEMS))
    early = EarlyGram(p, agb, gram, gram_rb, *sems.take(EARLY_SEMS))
    columns = RowGather(p, agb, PANEL, NEXT + 1, *sems.take(GATHER_SEMS))
    grams = RowGather(p, agb, GRAM, GRAM + 1, *sems.take(GATHER_SEMS))
    firsts = RowGather(p, agb, FIRST, FIRST + 1, *sems.take(GATHER_SEMS))
    prods = RowGather(p, agb, PROD, PROD + 1, *sems.take(GATHER_SEMS))
    reduce = RowReduce(p, part, rb_core, sums, rb_z, *sems.take(REDUCE_SEMS))

    panel.start()
    following.start()
    loop(NY - 1, lambda i: fetch(i + 1).wait())

    @pl.when(jnp.logical_and(p.r == 1, p.c == 0))
    def _():
        near_src[...] = a_ref[0].T

    first.start()

    def product(i, half):
        rows = pl.ds(half * (W // 2), W // 2)
        part[half * NZ:(half + 1) * NZ] += dot3(prow[i, rows], a_ref[i]).reshape(NZ, SUB, W)

    def products(*offsets):
        for d in offsets:
            product((p.y + d) % NY, 0)

        @pl.when(p.native)
        def _():
            for d in offsets:
                product((p.y + d) % NY, 1)

    part[...] = jnp.zeros_like(part)
    spread.own(home, lambda q: early.add(a_ref[q], q))
    early.start()
    panel.arrive()
    following.arrive()
    columns.start()
    spread.ring(1)
    early.along_x(first)
    products(0)
    spread.ring(2)
    early.along_l()
    columns.relay()
    products(1, 7)
    spread.ring(3)
    early.along_y()
    products(2, 6)
    spread.last()
    early.arrive()
    grams.start()
    firsts.start()
    products(3, 5, 4)

    @pl.when(jnp.logical_not(p.native))
    def _():
        def rest(t):
            i = (p.y + t) % NY
            spread.late(i)
            product(i, 1)

        loop(NY, rest)

    reduce.start()
    columns.finish()
    grams.relay()
    reduce.across()
    grams.finish()
    firsts.relay()

    y_ref[...] = agb[GRAM].reshape(W, W)
    row[...] = jnp.zeros_like(row)
    colsum = ColumnSums(p, *sum_bufs, *sems.take(SUM_SEMS), sems.take(GATHER_SEMS))
    images = Spread(p, irow, *sems.take(SPREAD_SEMS))

    def step(j):
        sweep(j, y_ref, m, row, lt)

        @pl.when(j == 0)
        def _():
            firsts.finish()
            m[...] = -agb[FIRST].reshape(W, W)

        @pl.when(j == 1)
        def _():
            total = reduce.total()
            agb[PROD, p.piece] = total
            prods.start()
            colsum.mine[0] = dot6(total, agb[PANEL].reshape(W, W), NT)
            colsum.mine[1] = jnp.where(p.c == 1, total, 0.0)
            colsum.mine[2] = jnp.where(p.c == 1, agb[NEXT, p.piece], 0.0)
            colsum.along_l()

        @pl.when(j == 3)
        def _():
            colsum.along_x()

        @pl.when(j == 4)
        def _():
            prods.relay()

        @pl.when(j == 5)
        def _():
            colsum.along_y()

        @pl.when(j == 8)
        def _():
            colsum.return_x()

    loop(9, step)
    prods.finish()

    it_ref[...] = agb[NEXT].reshape(W, W) - dot6(y_ref[...], agb[PROD].reshape(W, W))

    @pl.when(p.diag)
    def _():
        irow[p.y] = it_ref[...].T
        images.own(p.diag)

    colsum.along_row()
    shifted = jnp.where(p.c == 1, lt[...].T, 0.0) - agb[PANEL].reshape(W, W)
    r_ref[...] = dot6(m[...], shifted)

    @pl.when(jnp.logical_not(p.diag))
    def _():
        images.own(p.diag)

    k_ref[...] = dot6(m[...], lt[...], NT)

    def away(i, half):
        rows = pl.ds(half * (W // 2), W // 2)
        a_ref[i, rows] -= dot3(irow[i, rows], r_ref[...])

    def aways(*offsets):
        for d in offsets:
            away((p.y + d) % NY, 0)

        @pl.when(p.native)
        def _():
            for d in offsets:
                away((p.y + d) % NY, 1)

    def flip(i):
        prow[i] = prow[i].T

    spread.drain()
    images.ring(1)
    reduce.finish()
    early.finish()
    for each in (panel, following, first):
        each.finish()

    @pl.when(sends_home)
    def _():
        loop(NQ, lambda q: to_home(q).wait_send())

    loop(4, flip)
    aways(0)
    images.ring(2)
    colsum.gather.relay()
    loop(4, lambda i: flip(4 + i))
    aways(1, 7)
    images.ring(3)
    colsum.finish()
    aways(2, 6)
    images.last()
    aways(3, 5, 4)
    colsum.gather.finish()
    inv = y_ref[...]
    far = dot3(inv, r_ref[...], TN)
    prod = colsum.out[1].reshape(W, W)
    bent = dot3(inv, dot3(colsum.out[0].reshape(W, W), far) - dot3(prod, r_ref[...]))
    bent = bent + (dot3(colsum.out[2].reshape(W, W), r_ref[...]) - dot3(prod, far, TN))
    s_ref[...] = dot3(k_ref[...], it_ref[...] - bent, TN)
    u_ref[...] = dot3(inv, s_ref[...], TN)

    def update(t):
        i = (p.y + t) % NY
        images.late(i)

        @pl.when(jnp.logical_not(p.native))
        def _():
            away(i, 1)

        b = i * (NZ * NC) + p.r
        old = a_ref[i]
        new = old + dot3(prow[i], u_ref[...])
        out[i] = jnp.where(b == 1, new - s_ref[...], new)

        @pl.when(p.c == 0)
        def _():
            out[i] = jnp.where(b == 0, old, jnp.where(b == 1, lt[...], 0.0))

        @pl.when(jnp.logical_and(p.c > 0, b == 0))
        def _():
            out[i] = jnp.where(p.c == 1, lt[...].T, 0.0)

    loop(NY, update)
    images.drain()


def panel_call(slab):
    dma = pltpu.SemaphoreType.DMA
    square = pltpu.VMEM((W, W), F32)
    blocks = pltpu.VMEM((NY, W, W), F32)
    return pl.pallas_call(
        panel_kernel,
        out_shape=jax.ShapeDtypeStruct((NY, W, W), F32),
        in_specs=[pl.BlockSpec(memory_space=pl.ANY)],
        out_specs=pl.BlockSpec(memory_space=pltpu.VMEM),
        scratch_shapes=[blocks] * 3 + [square] * 7 + [
            pltpu.VMEM((5, 8, SUB, W), F32),
            square,
            square,
            pltpu.VMEM((8, SUB, W), F32),
            pltpu.VMEM((7, SUB, W), F32),
            square,
            pltpu.VMEM((SUB, W), F32),
        ] + REDUCE_BUFS + [dma((NY,))] + SUM_BUFS
        + SPREAD_SEMS + [dma((NQ,))] + SCATTER_SEMS * 3 + EARLY_SEMS + GATHER_SEMS * 4 + REDUCE_SEMS
        + SUM_SEMS + GATHER_SEMS + SPREAD_SEMS,
        compiler_params=pltpu.CompilerParams(
            collective_id=0, has_side_effects=True, vmem_limit_bytes=VMEM_LIMIT),
        name="panel_step",
    )(slab)


def on_device(matrix):
    slab = matrix.reshape(NY, W, W)
    return panel_call(slab).reshape(matrix.shape)


def solution(mesh):
    return jax.shard_map(
        on_device,
        mesh=mesh,
        in_specs=(P(None, "row", None, "col"),),
        out_specs=P(None, "row", None, "col"),
        check_vma=False,
    )
```

```python
import functools

import jax
import jax.numpy as jnp
from jax import lax
from jax.experimental import pallas as pl
from jax.experimental.pallas import tpu as pltpu
from jax.sharding import PartitionSpec as P

NY, NX, NZ, NL, NC = 8, 4, 4, 2, 2
W = 256
SUB = 32
NQ = 8
QR = W // NQ
GROUP = 8
F32, BF16 = jnp.float32, jnp.bfloat16
MESH = pl.DeviceIdType.MESH
VMEM_LIMIT = 50 * 1024 * 1024
NN = (((1,), (0,)), ((), ()))
NT = (((1,), (1,)), ((), ()))
TN = (((0,), (0,)), ((), ()))


def split2(v):
    hi = v.astype(BF16)
    return hi, (v - hi.astype(F32)).astype(BF16)


def split3(v):
    a = v.astype(BF16)
    rest = v - a.astype(F32)
    b = rest.astype(BF16)
    return a, b, (rest - b.astype(F32)).astype(BF16)


def mm(a, b, dims):
    return lax.dot_general(a, b, dims, preferred_element_type=F32)


def dot3(a, b, dims=NN):
    ah, al = split2(a)
    bh, bl = split2(b)
    return mm(ah, bh, dims) + (mm(ah, bl, dims) + mm(al, bh, dims))


def dot6(a, b, dims=NN):
    a1, a2, a3 = split3(a)
    b1, b2, b3 = split3(b)
    low = mm(a2, b2, dims) + (mm(a1, b3, dims) + mm(a3, b1, dims))
    return mm(a1, b1, dims) + ((mm(a1, b2, dims) + mm(a2, b1, dims)) + low)


def packed_tdot(a, b):
    a1, a2, a3 = split3(a)
    b1, b2, b3 = split3(b)
    left = jnp.concatenate([a1, a1, a2, a2, a1, a3], axis=0)
    right = jnp.concatenate([b1, b2, b1, b2, b3, b1], axis=0)
    return mm(left, right, TN)


def iota(shape, dim):
    return lax.broadcasted_iota(jnp.int32, shape, dim)


class Place:
    def __init__(self):
        self.r = lax.axis_index("row")
        self.c = lax.axis_index("col")
        self.z, self.h = self.r // NC, self.r % NC
        self.y, self.x, self.l = self.c // (NX * NL), (self.c // NL) % NX, self.c % NL
        self.piece = self.h * NZ + self.z
        self.native = self.l == self.h
        self.diag = jnp.logical_and(self.native, self.x == self.z)

    def at_y(self, d):
        return (self.r, ((self.y + d) % NY * NX + self.x) * NL + self.l)

    def at_x(self, d):
        return (self.r, (self.y * NX + (self.x + d) % NX) * NL + self.l)

    def at_l(self):
        return (self.r, (self.y * NX + self.x) * NL + (1 - self.l))

    def at_z(self, d):
        return (((self.z + d) % NZ) * NC + self.h, self.c)

    def at_core(self):
        return (self.z * NC + (1 - self.h), self.c)

    def at_row(self, d):
        return ((self.r + d) % (NZ * NC), self.c)


def rcopy(src, dst, send, recv, device):
    return pltpu.make_async_remote_copy(
        src_ref=src, dst_ref=dst, send_sem=send, recv_sem=recv, device_id=device, device_id_type=MESH
    )


def greet(devices):
    barrier = pltpu.get_barrier_semaphore()
    for device in devices:
        pl.semaphore_signal(barrier, inc=1, device_id=device, device_id_type=MESH)
    pl.semaphore_wait(barrier, len(devices))


def loop(n, body):
    def step(t, carry):
        body(t)
        return carry

    lax.fori_loop(0, n, step, 0)


class Spread:
    def __init__(self, place, buf, recv, send_x, send_y, send_l):
        self.p, self.buf, self.recv = place, buf, recv
        self.send_x, self.send_y, self.send_l = send_x, send_y, send_l

    def chunk(self, i, q):
        return self.buf.at[i, pl.ds(pl.multiple_of(q * QR, QR), QR)]

    def copy(self, i, q, send, device):
        part = self.chunk(i, q)
        return rcopy(part, part, send, self.recv.at[i, q], device)

    def to_x(self, d, q):
        return self.copy(self.p.y, q, self.send_x.at[d - 1], self.p.at_x(d))

    def to_y(self, side, s, q):
        sign = 1 if side == 0 else -1
        i = (self.p.y - sign * s + NY) % NY
        return self.copy(i, q, self.send_y.at[side, s], self.p.at_y(sign + NY))

    def to_l(self, i, q):
        return self.copy(i, q, self.send_l.at[i], self.p.at_l())

    def arrive(self, i, q):
        self.copy(i, q, self.send_l.at[i], self.p.at_l()).wait_recv()

    def own(self, home, beside=lambda q: None):
        p = self.p

        def body(q):
            @pl.when(jnp.logical_and(p.native, jnp.logical_not(home)))
            def _():
                self.arrive(p.y, q)

            @pl.when(jnp.logical_and(jnp.logical_not(p.native), q < NQ // 2))
            def _():
                self.arrive(p.y, q)

            @pl.when(p.diag)
            def _():
                for d in (1, 3, 2):
                    self.to_x(d, q).start()

            @pl.when(p.native)
            def _():
                self.to_l(p.y, q).start()

            @pl.when(jnp.logical_or(p.native, q < NQ // 2))
            def _():
                self.to_y(0, 0, q).start()
                self.to_y(1, 0, q).start()

            beside(q)

        loop(NQ, body)

    def sends_y(self, side, s, q):
        if s < 3:
            return jnp.logical_or(self.p.native, q < NQ // 2)
        if side == 0:
            return q < jnp.where(self.p.native, NQ // 2, NQ // 4)
        return jnp.where(self.p.native, q, (q % (NQ // 2)) * 2 * (q < NQ // 2)) >= NQ // 2

    def ring(self, s):
        p = self.p

        def body(q):
            for side in (0, 1):
                sign = 1 if side == 0 else -1
                i = (p.y - sign * s + NY) % NY

                @pl.when(jnp.logical_or(p.native, q < NQ // 2))
                def _(i=i):
                    self.arrive(i, q)

                @pl.when(self.sends_y(side, s, q))
                def _(side=side):
                    self.to_y(side, s, q).start()

                @pl.when(jnp.logical_and(p.native, q >= NQ // 2))
                def _(i=i):
                    self.to_l(i, q).start()

        loop(NQ, body)

    def last(self):
        p = self.p
        i = (p.y + 4) % NY

        def body(q):
            @pl.when(jnp.logical_or(p.native, q < NQ // 2))
            def _():
                self.arrive(i, q)

            @pl.when(jnp.logical_and(p.native, q >= NQ // 2))
            def _():
                self.to_l(i, q).start()

        loop(NQ, body)

    def late(self, i):
        @pl.when(jnp.logical_not(self.p.native))
        def _():
            loop(NQ // 2, lambda q: self.arrive(i, NQ // 2 + q))

    def sent(self, rows, send):
        part = self.buf.at[self.p.y, pl.ds(0, rows)]
        rcopy(part, part, send, self.recv.at[0, 0], self.p.at_l()).wait_send()

    def drain(self):
        p = self.p

        @pl.when(p.diag)
        def _():
            for d in range(3):
                self.sent(W, self.send_x.at[d])

        def ring(full):
            for side in (0, 1):
                for s in range(3):
                    self.sent(full, self.send_y.at[side, s])
                self.sent(full // 2, self.send_y.at[side, 3])

        @pl.when(p.native)
        def _():
            ring(W)
            self.sent(W, self.send_l.at[p.y])
            loop(NY - 1, lambda t: self.sent(W // 2, self.send_l.at[(p.y + 1 + t) % NY]))

        @pl.when(jnp.logical_not(p.native))
        def _():
            ring(W // 2)


SPREAD_SEMS = [
    pltpu.SemaphoreType.DMA((NY, NQ)),
    pltpu.SemaphoreType.DMA((3,)),
    pltpu.SemaphoreType.DMA((2, 4)),
    pltpu.SemaphoreType.DMA((NY,)),
]


class RowGather:
    def __init__(self, place, buf, lo, hi, recv, send):
        self.p, self.buf, self.lo, self.hi = place, buf, lo, hi
        self.recv, self.send = recv, send

    def copy(self, j, slot, device):
        part = self.buf.at[pl.ds(self.lo, self.hi - self.lo), j]
        return rcopy(part, part, self.send.at[slot], self.recv.at[j], device)

    def to_z(self, d):
        return self.copy(self.p.piece, d - 1, self.p.at_z(d))

    def to_core(self, d):
        j = self.p.h * NZ + (self.p.z - d + NZ) % NZ
        return self.copy(j, 3 + d, self.p.at_core())

    def start(self):
        for d in (1, 3, 2):
            self.to_z(d).start()
        self.to_core(0).start()

    def relay(self):
        for d in (1, 3, 2):
            self.to_core(d).wait_recv()
            self.to_core(d).start()

    def finish(self):
        for d in range(4):
            j = (1 - self.p.h) * NZ + (self.p.z - d + NZ) % NZ
            self.copy(j, 3 + d, self.p.at_core()).wait_recv()
        for d in (1, 2, 3):
            self.to_z(d).wait_send()
        for d in range(4):
            self.to_core(d).wait_send()


GATHER_SEMS = [pltpu.SemaphoreType.DMA((NZ * NC,)), pltpu.SemaphoreType.DMA((7,))]


def row_piece(r):
    return (r % NC) * NZ + r // NC


class RowScatter:
    def __init__(self, place, root, active, src, dst, recv, send):
        self.p, self.src, self.dst = place, src, dst
        self.recv, self.send = recv, send
        self.is_root = jnp.logical_and(place.r == root, active)
        self.is_leaf = jnp.logical_and(place.r != root, active)

    def copy(self, d):
        j = row_piece((self.p.r + d) % (NZ * NC))
        part = self.src.at[pl.ds(pl.multiple_of(j * SUB, SUB), SUB)]
        return rcopy(part, self.dst.at[j], self.send.at[d - 1], self.recv, self.p.at_row(d))

    def start(self):
        @pl.when(self.is_root)
        def _():
            for d in range(1, 8):
                self.copy(d).start()
            self.dst[self.p.piece] = self.src[pl.ds(pl.multiple_of(self.p.piece * SUB, SUB), SUB)]

    def arrive(self):
        @pl.when(self.is_leaf)
        def _():
            self.copy(1).wait_recv()

    def finish(self):
        @pl.when(self.is_root)
        def _():
            for d in range(1, 8):
                self.copy(d).wait_send()


SCATTER_SEMS = [pltpu.SemaphoreType.DMA(()), pltpu.SemaphoreType.DMA((7,))]

GRAM, FIRST, PROD, PANEL, NEXT = range(5)


class RowReduce:
    def __init__(self, place, part, rb_core, sums, rb_z, send_c, recv_c, send_z, recv_z):
        self.p, self.part, self.rb_core, self.sums, self.rb_z = place, part, rb_core, sums, rb_z
        self.send_z, self.recv_z = send_z, recv_z
        other = pl.ds(pl.multiple_of((1 - place.h) * NZ, NZ), NZ)
        self.out = rcopy(part.at[other], rb_core, send_c, recv_c, place.at_core())

    def to_z(self, d):
        p = self.p
        return rcopy(self.sums.at[(p.z + d) % NZ], self.rb_z.at[d - 1],
                     self.send_z.at[d - 1], self.recv_z.at[d - 1], p.at_z(d))

    def start(self):
        self.out.start()

    def across(self):
        self.out.wait_recv()
        mine = pl.ds(pl.multiple_of(self.p.h * NZ, NZ), NZ)
        self.sums[...] = self.part[mine] + self.rb_core[...]
        for d in (1, 3, 2):
            self.to_z(d).start()

    def total(self):
        total = self.sums[self.p.z]
        for d in (1, 3, 2):
            self.to_z(d).wait_recv()
            total = total + self.rb_z[d - 1]
        return total

    def finish(self):
        self.out.wait_send()
        for d in (1, 2, 3):
            self.to_z(d).wait_send()


REDUCE_BUFS = [
    pltpu.VMEM((8, SUB, W), F32),
    pltpu.VMEM((NZ, SUB, W), F32),
    pltpu.VMEM((NZ, SUB, W), F32),
    pltpu.VMEM((3, SUB, W), F32),
]
REDUCE_SEMS = [pltpu.SemaphoreType.DMA(()), pltpu.SemaphoreType.DMA(()),
               pltpu.SemaphoreType.DMA((3,)), pltpu.SemaphoreType.DMA((3,))]


class EarlyGram:
    def __init__(self, place, agb, gram, rb, send_r, recv_r, send_x, send_l, send_y, recv):
        self.p, self.agb, self.gram, self.rb = place, agb, gram, rb
        self.send_r, self.recv_r = send_r, recv_r
        self.send_x, self.send_l, self.send_y, self.recv = send_x, send_l, send_y, recv
        p = place
        self.root = p.c == 0
        self.on_x = jnp.logical_and(p.y == 0, p.l == 0)
        self.on_y = p.y == 0

    def scatter(self, d):
        j = row_piece((self.p.r + d) % (NZ * NC))
        return rcopy(self.gram.at[j], self.rb.at[d - 1], self.send_r.at[d - 1], self.recv_r.at[d - 1], self.p.at_row(d))

    def piece(self, send, device):
        part = self.agb.at[pl.ds(GRAM, 2), self.p.piece]
        return rcopy(part, part, send, self.recv, device)

    def to_x(self, d):
        return self.piece(self.send_x.at[d - 1], self.p.at_x(d))

    def to_l(self):
        return self.piece(self.send_l, self.p.at_l())

    def to_y(self, d):
        return self.piece(self.send_y.at[d - 1], self.p.at_y(d))

    def add(self, block, i):
        @pl.when(self.root)
        def _():
            mine = jnp.where(jnp.logical_and(i == 0, self.p.r == 0), 0.0, block)
            prod = dot3(mine.T, mine).reshape(8, SUB, W)
            self.gram[...] = jnp.where(i == 0, prod, self.gram[...] + prod)

    def start(self):
        @pl.when(self.root)
        def _():
            for d in range(1, 8):
                self.scatter(d).start()

    def along_x(self, first):
        @pl.when(self.root)
        def _():
            total = self.gram[self.p.piece]
            for d in range(1, 8):
                self.scatter(d).wait_recv()
                total = total + self.rb[d - 1]
            self.agb[GRAM, self.p.piece] = total
        first.arrive()

        @pl.when(self.root)
        def _():
            for d in (1, 3, 2):
                self.to_x(d).start()

    def along_l(self):
        @pl.when(jnp.logical_and(self.on_x, self.p.x != 0))
        def _():
            self.to_l().wait_recv()

        @pl.when(self.on_x)
        def _():
            self.to_l().start()

    def along_y(self):
        @pl.when(jnp.logical_and(self.on_y, self.p.l != 0))
        def _():
            self.to_l().wait_recv()

        @pl.when(self.on_y)
        def _():
            for d in (4, 3, 5, 2, 6, 1, 7):
                self.to_y(d).start()

    def arrive(self):
        @pl.when(jnp.logical_not(self.on_y))
        def _():
            self.to_l().wait_recv()

    def finish(self):
        @pl.when(self.root)
        def _():
            for d in range(1, 8):
                self.scatter(d).wait_send()
            for d in (1, 2, 3):
                self.to_x(d).wait_send()

        @pl.when(self.on_x)
        def _():
            self.to_l().wait_send()

        @pl.when(self.on_y)
        def _():
            for d in range(1, 8):
                self.to_y(d).wait_send()


EARLY_SEMS = [pltpu.SemaphoreType.DMA((7,)), pltpu.SemaphoreType.DMA((7,)), pltpu.SemaphoreType.DMA((3,)),
              pltpu.SemaphoreType.DMA(()), pltpu.SemaphoreType.DMA((7,)), pltpu.SemaphoreType.DMA(())]


def pivot(t, p0, p1, cols, lane, row, jordan):
    col = cols[0]
    inv = 1.0 / col[t:t + 1, :]
    r0 = jnp.where(lane[t:t + 1] == t, 1.0, p0[t:t + 1]) * inv
    r1 = p1[t:t + 1] * inv
    here = row == t
    apply = jnp.logical_not(here) if jordan else row > t
    factor = jnp.where(apply, col, 0.0)
    rest = []
    for other in cols[1:]:
        ro = other[t:t + 1] * inv
        new = other - factor * ro
        rest.append(jnp.where(here, ro, new) if jordan else new)
    p0 = jnp.where(jnp.logical_and(apply, lane == t), 0.0, p0) - factor * r0
    p1 = p1 - factor * r1
    if jordan:
        p0, p1 = jnp.where(here, r0, p0), jnp.where(here, r1, p1)
    return p0, p1, rest


def group_columns(p0, t):
    return [jnp.broadcast_to(p0[:, u:u + 1], (SUB, 128)) for u in range(t, t + GROUP)]


def turn(v):
    return jnp.concatenate([v[:, SUB:], v[:, :SUB]], axis=1)


def turn_store(ref, body, panel):
    out = turn(body)
    ref[:W - SUB, :] = out[SUB:]
    ref[W - SUB:, :] = turn(panel)


def sweep(j, t_ref, m_ref, row_ref, lt_ref):
    lane = iota((SUB, 128), 1)
    row = iota((SUB, 128), 0)
    lane2 = iota((SUB, W), 1)
    before = row_ref[...]
    m_left = m_ref[:, :128].T[:SUB] + before
    q0 = m_ref[:SUB, :128] + jnp.where(lane < SUB, jnp.concatenate(
        [before[:, :SUB].T, jnp.zeros((SUB, 128 - SUB), F32)], axis=1), 0.0)
    q1 = m_ref[:SUB, 128:]
    p0, p1 = t_ref[:SUB, :128], t_ref[:SUB, 128:]
    for t in range(SUB):
        if t % GROUP == 0:
            p_cols, q_cols = group_columns(p0, t), group_columns(q0, t)
        p0, p1, p_cols = pivot(t, p0, p1, p_cols, lane, row, False)
        q0, q1, q_cols = pivot(t, q0, q1, q_cols, lane, row, True)

    diag = jnp.sum(jnp.where(lane == row, p0, 0.0), axis=1, keepdims=True)
    scale = 1.0 / jnp.sqrt(diag)
    p0, p1 = p0 * scale, p1 * scale
    upper = jnp.where(lane >= row, p0, 0.0)
    inside = jnp.where(lane < row, p0, jnp.where(lane == row, scale, 0.0))
    table = jnp.concatenate([jnp.where(lane < SUB, inside, p0), p1], axis=1)
    live = jnp.logical_and(lane2 < SUB * (8 - j), lane2 >= 0)
    upper = jnp.where(live, jnp.concatenate([upper, p1], axis=1), 0.0)
    first = iota((W, W), 1) < SUB
    t_new = jnp.where(first, 0.0, t_ref[...]) - packed_tdot(jnp.where(lane2 < SUB, 0.0, upper), table)
    panel = jnp.concatenate([q0, q1], axis=1)
    m_new = jnp.where(first, 0.0, m_ref[...]) - packed_tdot(m_left, panel)

    @pl.when(j < 8)
    def _():
        turn_store(t_ref, t_new, table)
        row_ref[...] = upper
        lt_ref[pl.ds(pl.multiple_of(j * SUB, SUB), SUB), :] = pltpu.roll(upper, j * SUB, 1)

    @pl.when(j > 0)
    def _():
        turn_store(m_ref, m_new, panel)


class ColumnSums:
    def __init__(self, place, out, mine, s1, s2, s3, rows, rb1, rb2, rb3, c1, c2, c3, c4, gather):
        self.p, self.out, self.mine, self.rows = place, out, mine, rows
        self.s1, self.s2, self.s3 = s1, s2, s3
        self.rb1, self.rb2, self.rb3 = rb1, rb2, rb3
        self.c1, self.c2, self.c3, self.c4 = c1, c2, c3, c4
        self.gather = RowGather(place, out, 0, 3, *gather)
        self.here = pl.ds(pl.multiple_of(place.x * 8, 8), 8)

    def to_l(self):
        return rcopy(self.mine, self.rb1, self.c1.at[0], self.c1.at[1], self.p.at_l())

    def to_x(self, d):
        x = (self.p.x + d) % NX
        part = self.s1.at[:, pl.ds(pl.multiple_of(x * 8, 8), 8)]
        return rcopy(part, self.rb2.at[d - 1], self.c2.at[0, d - 1], self.c2.at[1, d - 1], self.p.at_x(d))

    def to_y(self, d):
        return rcopy(self.s2, self.rb3.at[d - 1], self.c3.at[0, d - 1], self.c3.at[1, d - 1], self.p.at_y(d))

    def back_x(self, d):
        part = self.rows.at[:, self.here]
        return rcopy(self.s3, part, self.c4.at[0, d - 1], self.c4.at[1, d - 1], self.p.at_x(d))

    def along_l(self):
        self.to_l().start()

    def along_x(self):
        self.to_l().wait_recv()
        self.s1[...] = self.mine[...] + self.rb1[...]
        for d in (1, 3, 2):
            self.to_x(d).start()

    def along_y(self):
        total = self.s1[:, self.here]
        for d in (1, 2, 3):
            self.to_x(d).wait_recv()
            total = total + self.rb2[d - 1]
        self.s2[...] = total
        for d in (4, 3, 5, 2, 6, 1, 7):
            self.to_y(d).start()

    def return_x(self):
        total = self.s2[...]
        for d in range(1, 8):
            self.to_y(d).wait_recv()
            total = total + self.rb3[d - 1]
        self.s3[...] = total
        self.rows[:, self.here] = total
        for d in (1, 3, 2):
            self.back_x(d).start()

    def along_row(self):
        for d in (1, 2, 3):
            self.back_x(d).wait_recv()
        self.out[:, self.p.piece] = self.rows[...]
        self.gather.start()

    def finish(self):
        self.to_l().wait_send()
        for d in (1, 2, 3):
            self.to_x(d).wait_send()
            self.back_x(d).wait_send()
        for d in range(1, 8):
            self.to_y(d).wait_send()


SUM_BUFS = [pltpu.VMEM((3, 8, SUB, W), F32), pltpu.VMEM((3, SUB, W), F32), pltpu.VMEM((3, SUB, W), F32),
            pltpu.VMEM((3, 8, W), F32), pltpu.VMEM((3, 8, W), F32), pltpu.VMEM((3, SUB, W), F32),
            pltpu.VMEM((3, SUB, W), F32), pltpu.VMEM((3, 3, 8, W), F32), pltpu.VMEM((7, 3, 8, W), F32)]
SUM_SEMS = [pltpu.SemaphoreType.DMA((2,)), pltpu.SemaphoreType.DMA((2, 3)),
            pltpu.SemaphoreType.DMA((2, 7)), pltpu.SemaphoreType.DMA((2, 3))]


class Sems:
    def __init__(self, refs):
        self.refs, self.at = refs, 0

    def take(self, group):
        self.at += len(group)
        return self.refs[self.at - len(group):self.at]


def panel_kernel(a_hbm, out, a_ref, prow, irow, lt, y_ref, k_ref, it_ref, r_ref, s_ref, u_ref, agb, src, near_src, gram, gram_rb, m, row, part, rb_core, sums, rb_z, load, *refs):
    sems = Sems(refs)
    sum_bufs = sems.take(SUM_BUFS)
    p = Place()

    def fetch(i):
        return pltpu.make_async_copy(a_hbm.at[i], a_ref.at[i], load.at[i])

    loop(NY, lambda i: fetch(i).start())
    greet([p.at_row(d) for d in range(1, 8)] + [p.at_y(d) for d in range(1, 8)] + [p.at_l()]
          + [p.at_x(d) for d in (1, 2, 3)])
    fetch(0).wait()

    spread_sems = sems.take(SPREAD_SEMS)
    spread = Spread(p, prow, *spread_sems)
    home_row = p.x * NC + p.l
    home = jnp.logical_and(p.diag, p.r == 0)

    @pl.when(p.r == 0)
    def _():
        src[...] = jnp.where(p.c == 0, 0.0, a_ref[0])

    @pl.when(p.r == 1)
    def _():
        src[...] = a_ref[0]

    home_sem = sems.take([0])[0]

    def to_home(q):
        rows = pl.ds(pl.multiple_of(q * QR, QR), QR)
        return rcopy(src.at[rows], prow.at[p.y, rows], home_sem.at[q], spread_sems[0].at[p.y, q], (home_row, p.c))

    @pl.when(home)
    def _():
        prow[p.y] = src[...]

    sends_home = jnp.logical_and(p.r == 0, home_row != 0)

    @pl.when(sends_home)
    def _():
        loop(NQ, lambda q: to_home(q).start())

    panel = RowScatter(p, 0, p.c >= 0, src, agb.at[PANEL], *sems.take(SCATTER_SEMS))
    following = RowScatter(p, 1, p.c >= 0, src, agb.at[NEXT], *sems.take(SCATTER_SEMS))
    first = RowScatter(p, 1, p.c == 0, near_src, agb.at[FIRST], *sems.take(SCATTER_SEMS))
    early = EarlyGram(p, agb, gram, gram_rb, *sems.take(EARLY_SEMS))
    columns = RowGather(p, agb, PANEL, NEXT + 1, *sems.take(GATHER_SEMS))
    grams = RowGather(p, agb, GRAM, GRAM + 1, *sems.take(GATHER_SEMS))
    firsts = RowGather(p, agb, FIRST, FIRST + 1, *sems.take(GATHER_SEMS))
    prods = RowGather(p, agb, PROD, PROD + 1, *sems.take(GATHER_SEMS))
    reduce = RowReduce(p, part, rb_core, sums, rb_z, *sems.take(REDUCE_SEMS))

    panel.start()
    following.start()
    loop(NY - 1, lambda i: fetch(i + 1).wait())

    @pl.when(jnp.logical_and(p.r == 1, p.c == 0))
    def _():
        near_src[...] = a_ref[0].T

    first.start()

    def product(i, half):
        rows = pl.ds(half * (W // 2), W // 2)
        part[half * NZ:(half + 1) * NZ] += dot3(prow[i, rows], a_ref[i]).reshape(NZ, SUB, W)

    def products(*offsets):
        for d in offsets:
            product((p.y + d) % NY, 0)

        @pl.when(p.native)
        def _():
            for d in offsets:
                product((p.y + d) % NY, 1)

    part[...] = jnp.zeros_like(part)
    spread.own(home, lambda q: early.add(a_ref[q], q))
    early.start()
    panel.arrive()
    following.arrive()
    columns.start()
    spread.ring(1)
    early.along_x(first)
    products(0)
    spread.ring(2)
    early.along_l()
    columns.relay()
    products(1, 7)
    spread.ring(3)
    early.along_y()
    products(2, 6)
    spread.last()
    early.arrive()
    grams.start()
    firsts.start()
    products(3, 5, 4)

    @pl.when(jnp.logical_not(p.native))
    def _():
        def rest(t):
            i = (p.y + t) % NY
            spread.late(i)
            product(i, 1)

        loop(NY, rest)

    reduce.start()
    columns.finish()
    grams.relay()
    reduce.across()
    grams.finish()
    firsts.relay()

    y_ref[...] = agb[GRAM].reshape(W, W)
    row[...] = jnp.zeros_like(row)
    colsum = ColumnSums(p, *sum_bufs, *sems.take(SUM_SEMS), sems.take(GATHER_SEMS))
    images = Spread(p, irow, *sems.take(SPREAD_SEMS))

    def step(j):
        sweep(j, y_ref, m, row, lt)

        @pl.when(j == 0)
        def _():
            firsts.finish()
            m[...] = -agb[FIRST].reshape(W, W)

        @pl.when(j == 1)
        def _():
            total = reduce.total()
            agb[PROD, p.piece] = total
            prods.start()
            colsum.mine[0] = dot6(total, agb[PANEL].reshape(W, W), NT)
            colsum.mine[1] = jnp.where(p.c == 1, total, 0.0)
            colsum.mine[2] = jnp.where(p.c == 1, agb[NEXT, p.piece], 0.0)
            colsum.along_l()

        @pl.when(j == 3)
        def _():
            colsum.along_x()

        @pl.when(j == 4)
        def _():
            prods.relay()

        @pl.when(j == 5)
        def _():
            colsum.along_y()

        @pl.when(j == 8)
        def _():
            colsum.return_x()

    loop(9, step)
    prods.finish()

    it_ref[...] = agb[NEXT].reshape(W, W) - dot6(y_ref[...], agb[PROD].reshape(W, W))

    @pl.when(p.diag)
    def _():
        irow[p.y] = it_ref[...].T
        images.own(p.diag)

    colsum.along_row()
    @pl.when(jnp.logical_not(p.diag))
    def _():
        images.own(p.diag)

    shifted = jnp.where(p.c == 1, lt[...].T, 0.0) - agb[PANEL].reshape(W, W)
    r_ref[...] = dot6(m[...], shifted)

    k_ref[...] = dot6(m[...], lt[...], NT)

    def away(i, half):
        rows = pl.ds(half * (W // 2), W // 2)
        a_ref[i, rows] -= dot3(irow[i, rows], r_ref[...])

    def aways(*offsets):
        for d in offsets:
            away((p.y + d) % NY, 0)

        @pl.when(p.native)
        def _():
            for d in offsets:
                away((p.y + d) % NY, 1)

    def flip(i):
        prow[i] = prow[i].T

    spread.drain()
    images.ring(1)
    reduce.finish()
    early.finish()
    for each in (panel, following, first):
        each.finish()

    @pl.when(sends_home)
    def _():
        loop(NQ, lambda q: to_home(q).wait_send())

    loop(4, flip)
    aways(0)
    images.ring(2)
    colsum.gather.relay()
    loop(4, lambda i: flip(4 + i))
    aways(1, 7)
    images.ring(3)
    colsum.finish()
    aways(2, 6)
    images.last()
    aways(3, 5, 4)
    colsum.gather.finish()
    inv = y_ref[...]
    far = dot3(inv, r_ref[...], TN)
    prod = colsum.out[1].reshape(W, W)
    bent = dot3(inv, dot3(colsum.out[0].reshape(W, W), far) - dot3(prod, r_ref[...]))
    bent = bent + (dot3(colsum.out[2].reshape(W, W), r_ref[...]) - dot3(prod, far, TN))
    s_ref[...] = dot3(k_ref[...], it_ref[...] - bent, TN)
    u_ref[...] = dot3(inv, s_ref[...], TN)

    def update(t):
        i = (p.y + t) % NY
        images.late(i)

        @pl.when(jnp.logical_not(p.native))
        def _():
            away(i, 1)

        b = i * (NZ * NC) + p.r
        old = a_ref[i]
        new = old + dot3(prow[i], u_ref[...])
        out[i] = jnp.where(b == 1, new - s_ref[...], new)

        @pl.when(p.c == 0)
        def _():
            out[i] = jnp.where(b == 0, old, jnp.where(b == 1, lt[...], 0.0))

        @pl.when(jnp.logical_and(p.c > 0, b == 0))
        def _():
            out[i] = jnp.where(p.c == 1, lt[...].T, 0.0)

    loop(NY, update)
    images.drain()


def panel_call(slab):
    dma = pltpu.SemaphoreType.DMA
    square = pltpu.VMEM((W, W), F32)
    blocks = pltpu.VMEM((NY, W, W), F32)
    return pl.pallas_call(
        panel_kernel,
        out_shape=jax.ShapeDtypeStruct((NY, W, W), F32),
        in_specs=[pl.BlockSpec(memory_space=pl.ANY)],
        out_specs=pl.BlockSpec(memory_space=pltpu.VMEM),
        scratch_shapes=[blocks] * 3 + [square] * 7 + [
            pltpu.VMEM((5, 8, SUB, W), F32),
            square,
            square,
            pltpu.VMEM((8, SUB, W), F32),
            pltpu.VMEM((7, SUB, W), F32),
            square,
            pltpu.VMEM((SUB, W), F32),
        ] + REDUCE_BUFS + [dma((NY,))] + SUM_BUFS
        + SPREAD_SEMS + [dma((NQ,))] + SCATTER_SEMS * 3 + EARLY_SEMS + GATHER_SEMS * 4 + REDUCE_SEMS
        + SUM_SEMS + GATHER_SEMS + SPREAD_SEMS,
        compiler_params=pltpu.CompilerParams(
            collective_id=0, has_side_effects=True, vmem_limit_bytes=VMEM_LIMIT),
        name="panel_step",
    )(slab)


def on_device(matrix):
    slab = matrix.reshape(NY, W, W)
    return panel_call(slab).reshape(matrix.shape)


def solution(mesh):
    return jax.shard_map(
        on_device,
        mesh=mesh,
        in_specs=(P(None, "row", None, "col"),),
        out_specs=P(None, "row", None, "col"),
        check_vma=False,
    )
```
